32 devices in a mesh: mem: 4 (over y, x), space: 8 (over z, core).
Axes of the slice: x: 2, y: 2, z: 4, core: 2. Of those that a mesh axis runs over, the one named last changes fastest.
Arguments:
- ensemble: bfloat16 [16, 16, 92160], P('mem', None, 'space'), may hold values from -100 to 100
- cotangent: bfloat16 [16, 16, 92160], P('mem', None, 'space'), may hold values from -6 to 6
- w_query: bfloat16 [16, 16], replicated, may hold values from -2 to 2
- w_key: bfloat16 [16, 16], replicated, may hold values from -2 to 2
- w_value: bfloat16 [16, 16], replicated, may hold values from -1.5 to 1.5
- w_out: bfloat16 [16, 16], replicated, may hold values from -1.5 to 1.5
Outputs:
- updated: float32 [16, 16, 92160], P('mem', None, 'space')
- ensemble_grad: float32 [16, 16, 92160], P('mem', None, 'space')
The draws below stay inside these ranges and needn't reach their ends.
All inputs are finite; a program needn't handle non-finite values.
Results may differ from the reference program's by a relative error of at most 0.0044.
Values may be sent and summed in bfloat16 or wider, within the bound.
No kernel may reach another device: no remote copies, remote signals or barrier semaphores. Data moves between devices by JAX's collectives and lax.ppermute only.
A program may use at most 128 MiB of HBM per device.

```python
import math
import jax
import jax.numpy as jnp
from jax import lax

CH = 16
NLON = 1440
LAT_DEV = 8
MEMBERS = 16
NLAT = 64
CELLS = 92160
N_SPACE = 8


def weight_pair(key):
    shared = jax.random.normal(jax.random.fold_in(key, 101), (CH, CH), jnp.float32) / math.sqrt(CH)
    partner = jax.random.normal(jax.random.fold_in(key, 102), (CH, CH), jnp.float32) / math.sqrt(CH)
    return (shared, partner)


def key_matrix(key):
    shared, partner = weight_pair(key)
    blended = 0.4 * shared + 0.9 * partner
    return blended


def value_pair(key):
    value_w = jnp.clip(jax.random.normal(jax.random.fold_in(key, 103), (CH, CH), jnp.float32), -6.0, 6.0) / math.sqrt(CH)
    out_w = jnp.clip(jax.random.normal(jax.random.fold_in(key, 104), (CH, CH), jnp.float32), -6.0, 6.0) / math.sqrt(CH)
    return (value_w, out_w)


def draw_w_query(key, part):
    shared, partner = weight_pair(key)
    return shared.astype(jnp.bfloat16)


def draw_w_key(key, part):
    return key_matrix(key).astype(jnp.bfloat16)


def draw_w_value(key, part):
    value_w, out_w = value_pair(key)
    return value_w.astype(jnp.bfloat16)


def draw_w_out(key, part):
    value_w, out_w = value_pair(key)
    return out_w.astype(jnp.bfloat16)


def ensemble_field(key):
    regions = NLAT // LAT_DEV
    noise = jax.random.normal(jax.random.fold_in(key, 1), (MEMBERS, CH, NLAT, NLON), jnp.float32)
    common = jax.random.normal(jax.random.fold_in(key, 2), (MEMBERS, MEMBERS), jnp.float32) / math.sqrt(MEMBERS)
    regional = jax.random.normal(jax.random.fold_in(key, 3), (regions, MEMBERS, MEMBERS), jnp.float32) / math.sqrt(MEMBERS)
    mixing = 0.25 * jnp.eye(MEMBERS, dtype=jnp.float32)[None] + 0.5 * common[None] + 0.9 * regional
    row_mixing = jnp.repeat(mixing, LAT_DEV, axis=0)
    latitude = jnp.arange(NLAT, dtype=jnp.float32) / max(NLAT - 1, 1)
    rising = 1.0 + 0.8 * latitude
    field = jnp.einsum('lmk,kcln->mcln', row_mixing, noise) * rising[None, None, :, None]
    return jnp.clip(field, -100.0, 100.0)


def draw_ensemble(key, part):
    field = ensemble_field(key)
    return field.reshape(MEMBERS, CH, NLAT * NLON).astype(jnp.bfloat16)


def draw_cotangent(key, part):
    field = ensemble_field(key)
    value_w, out_w = value_pair(key)
    mixer = jnp.dot(out_w.astype(jnp.bfloat16).astype(jnp.float32), value_w.astype(jnp.bfloat16).astype(jnp.float32), precision=lax.Precision.HIGHEST)
    echo = jnp.einsum('cd,mdln->mcln', mixer, field)
    noise = jax.random.normal(jax.random.fold_in(key, 6), (MEMBERS, CH, NLAT, NLON), jnp.float32)
    result = jnp.clip(noise + 0.2 * (field + echo), -6.0, 6.0)
    return result.reshape(MEMBERS, CH, NLAT * NLON).astype(jnp.bfloat16)


def setup_inputs(seed: int = 0) -> dict:
    streams_of = jax.random.split(jax.random.key(seed), 7)
    ensemble = draw_ensemble(jax.random.fold_in(streams_of[6], 71), 0)
    cotangent = draw_cotangent(jax.random.fold_in(streams_of[6], 71), 0)
    w_query = draw_w_query(jax.random.fold_in(streams_of[6], 71), 0)
    w_key = draw_w_key(jax.random.fold_in(streams_of[6], 71), 0)
    w_value = draw_w_value(jax.random.fold_in(streams_of[6], 71), 0)
    w_out = draw_w_out(jax.random.fold_in(streams_of[6], 71), 0)
    return dict(ensemble=ensemble, cotangent=cotangent, w_query=w_query, w_key=w_key, w_value=w_value, w_out=w_out)


def project(weight, field):
    return jnp.einsum('cd,mdp->mcp', weight.astype(jnp.float32), field.astype(jnp.float32))

def project_back(weight, field):
    return jnp.einsum('cd,mcp->mdp', weight.astype(jnp.float32), field.astype(jnp.float32))

def flatten(field):
    return field.reshape(field.shape[0], field.shape[1] * field.shape[2])

def pair_sum(left, right):
    return lax.dot_general(flatten(left), flatten(right), (((1,), (1,)), ((), ())), preferred_element_type=jnp.float32)

def normalize(scores):
    row_peak = lax.optimization_barrier(jnp.max(scores, axis=1, keepdims=True))
    exponent = jnp.exp(scores - row_peak)
    return exponent / lax.optimization_barrier(jnp.sum(exponent, axis=1, keepdims=True))

def combine(weights_half, field):
    mixed = jnp.dot(weights_half, flatten(field), preferred_element_type=jnp.float32)
    return mixed.astype(jnp.bfloat16).reshape(field.shape)

def reference(ensemble, cotangent, w_query, w_key, w_value, w_out):
    band = LAT_DEV * NLON

    def block(field, index):
        start = (index * band).astype(jnp.int32)
        return lax.dynamic_slice_in_dim(field, start, band, 2)

    def projections(index):
        piece = block(ensemble, index)
        grad_piece = block(cotangent, index)
        queries = project(w_query, piece).astype(jnp.bfloat16)
        key_field = project(w_key, piece).astype(jnp.bfloat16)
        value_field = project(w_value, piece).astype(jnp.bfloat16)
        grad_mixed = project_back(w_out, grad_piece).astype(jnp.bfloat16)
        return (piece, grad_piece, queries, key_field, value_field, grad_mixed)

    def gather_sums(index, carry):
        outcome = projections(index)
        return (carry[0] + pair_sum(outcome[2], outcome[3]), carry[1] + pair_sum(outcome[5], outcome[4]))
    zeros_pair = jnp.zeros((MEMBERS, MEMBERS), jnp.float32)
    total_scores, total_pairs = lax.fori_loop(0, N_SPACE, gather_sums, (zeros_pair, zeros_pair))
    score_scale = 1.0 / (CELLS * math.sqrt(CH))
    weights = normalize(score_scale * total_scores)
    weights_half = weights.astype(jnp.bfloat16)
    grad_scores = weights * (total_pairs - lax.optimization_barrier(jnp.sum(weights * total_pairs, axis=1, keepdims=True)))
    grad_scaled = (score_scale * grad_scores).astype(jnp.bfloat16)

    def finish(index, carry):
        updated, ensemble_grad = carry
        piece, grad_piece, queries, key_field, value_field, grad_mixed = projections(index)
        mixed = combine(weights_half, value_field)
        branch = project(w_out, mixed).astype(jnp.bfloat16)
        grad_queries = combine(grad_scaled, key_field)
        grad_keys = combine(grad_scaled.T, queries)
        grad_values = combine(weights_half.T, grad_mixed)
        grad_branch = (project_back(w_query, grad_queries) + project_back(w_key, grad_keys) + project_back(w_value, grad_values)).astype(jnp.bfloat16)
        out_block = piece.astype(jnp.float32) + branch.astype(jnp.float32)
        grad_block = grad_piece.astype(jnp.float32) + grad_branch.astype(jnp.float32)
        start = (index * band).astype(jnp.int32)
        updated = lax.dynamic_update_slice_in_dim(updated, out_block, start, 2)
        ensemble_grad = lax.dynamic_update_slice_in_dim(ensemble_grad, grad_block, start, 2)
        return (updated, ensemble_grad)
    empty = jnp.zeros((MEMBERS, CH, CELLS), jnp.float32)
    updated, ensemble_grad = lax.fori_loop(0, N_SPACE, finish, (empty, empty))
    return (updated, ensemble_grad)
```

```python
import functools
import math

import jax
import jax.numpy as jnp
from jax import lax
from jax.experimental import pallas as pl
from jax.experimental.pallas import tpu as pltpu
from jax.sharding import PartitionSpec as P

LANES = 128
HIGH = lax.Precision.HIGHEST
VMEM = pltpu.MemorySpace.VMEM


def mm(a, b, dims, precision=None):
    return lax.dot_general(
        a, b, (dims, ((), ())), precision=precision, preferred_element_type=jnp.float32
    )


def chunk_start(index, chunk, length):
    return pl.multiple_of(jnp.minimum(index * chunk, length - chunk), LANES)


def partner(me, step):
    return me ^ step


def lane_tiles(width, step=512):
    return [(at, min(step, width - at)) for at in range(0, width, step)]


def member_of_row(me, rows, channels, members, group):
    row = lax.broadcasted_iota(jnp.int32, (rows, members), 0)
    col = lax.broadcasted_iota(jnp.int32, (rows, members), 1)
    per_group = group * channels
    owner = (row // per_group) ^ me
    member = owner * group + (row % per_group) // channels
    return (member == col).astype(jnp.float32)


def split_kernel(me_of, count, chunk, length, x_ref, *rest):
    outs, sem = rest[:count], rest[count]
    me = me_of()
    copies = [
        pltpu.make_async_copy(
            x_ref.at[:, pl.ds(chunk_start(partner(me, s), chunk, length), chunk)],
            outs[s],
            sem.at[s],
        )
        for s in range(count)
    ]
    for copy in copies:
        copy.start()
    for copy in copies:
        copy.wait()


def tiled(small, rows, channels):
    tall = jnp.concatenate([small] * (rows // channels), axis=0)
    col = lax.broadcasted_iota(jnp.int32, (channels, rows), 1)
    row = lax.broadcasted_iota(jnp.int32, (channels, rows), 0)
    spread = (col % channels == row).astype(jnp.float32)
    return mm(tall, spread, ((1,), (0,)), HIGH)


def split_weights_kernel(
    me_of, count, chunk, length, rows, channels,
    x_ref, dep_ref, wq_ref, wk_ref, wv_ref, wo_ref, *rest,
):
    outs = rest[:count]
    qk_ref, qkt_ref, ov_ref, ovt_ref, sem = rest[count:]
    me = me_of()
    copies = [
        pltpu.make_async_copy(
            x_ref.at[:, pl.ds(chunk_start(partner(me, s), chunk, length), chunk)],
            outs[s],
            sem.at[s],
        )
        for s in range(count)
    ]
    for copy in copies:
        copy.start()
    wq, wk = wq_ref[...].astype(jnp.float32), wk_ref[...].astype(jnp.float32)
    wv, wo = wv_ref[...].astype(jnp.float32), wo_ref[...].astype(jnp.float32)
    wqt, wkt, wvt, wot = wq.T, wk.T, wv.T, wo.T
    qk_ref[...] = tiled(mm(wqt, wk, ((1,), (0,)), HIGH), rows, channels)
    qkt_ref[...] = tiled(mm(wkt, wq, ((1,), (0,)), HIGH), rows, channels)
    ov_ref[...] = tiled(mm(wo, wv, ((1,), (0,)), HIGH), rows, channels)
    ovt_ref[...] = tiled(mm(wvt, wot, ((1,), (0,)), HIGH), rows, channels)
    for copy in copies:
        copy.wait()


def gather_tile(refs, at, width):
    return jnp.concatenate([r[:, at:at + width] for r in refs], axis=0)


def fold(weighted, picks):
    half = mm(weighted, picks, ((1,), (0,)), HIGH)
    return mm(picks, half, ((0,), (0,)), HIGH)


def gram_kernel(me_of, count, chunk, length, group, channels, members, same, *refs):
    me = me_of()
    left = refs[:count]
    right = left if same else refs[count:2 * count]
    tile_ref, out_ref = refs[-2], refs[-1]
    rows = count * left[0].shape[0]
    skip = me * chunk - chunk_start(me, chunk, length)
    total = jnp.zeros((rows, rows), jnp.float32)
    for at, width in lane_tiles(chunk):
        b = gather_tile(right, at, width)
        a = b if same else gather_tile(left, at, width)
        lane = lax.broadcasted_iota(jnp.int32, (rows, width), 1) + at
        a = jnp.where(lane >= skip, a.astype(jnp.float32), 0.0).astype(jnp.bfloat16)
        total = total + mm(a, b, ((1,), (1,)))
    picks = member_of_row(me, rows, channels, members, group)
    out_ref[...] = fold(total * tile_ref[...], picks)


def softmax(scores):
    peak = jnp.max(scores, axis=1, keepdims=True)
    exponent = jnp.exp(scores - peak)
    return exponent / jnp.sum(exponent, axis=1, keepdims=True)


def spread(small, picks):
    tall = mm(picks, small.astype(jnp.bfloat16), ((1,), (0,))).astype(jnp.bfloat16)
    return mm(tall, picks, ((1,), (1,)))


def spread_t(small, picks):
    tall = mm(picks, small.astype(jnp.bfloat16), ((1,), (1,))).astype(jnp.bfloat16)
    return mm(tall, picks, ((1,), (1,)))


def two_parts(value):
    high = value.astype(jnp.bfloat16)
    return high, (value - high.astype(jnp.float32)).astype(jnp.bfloat16)


def branch_kernel(me_of, count, chunk, group, channels, members, scale, s_ref, ov_ref, *refs):
    me = me_of()
    fields, outs = refs[:count], refs[count:]
    per = fields[0].shape[0]
    rows = count * per
    picks = member_of_row(me, rows, channels, members, group).astype(jnp.bfloat16)
    weights = softmax(s_ref[...] * scale)
    high, low = two_parts(spread(weights, picks) * ov_ref[...])
    for at, width in lane_tiles(chunk):
        e = gather_tile(fields, at, width)
        b = (mm(high, e, ((1,), (0,))) + mm(low, e, ((1,), (0,)))).astype(jnp.bfloat16)
        for s in range(count):
            outs[s][:, at:at + width] = b[s * per:(s + 1) * per]


def grad_kernel(
    me_of, count, chunk, group, channels, members, scale,
    s_ref, p_ref, qk_ref, qkt_ref, ovt_ref, *refs,
):
    me = me_of()
    fields, grads, outs = refs[:count], refs[count:2 * count], refs[2 * count:]
    per = fields[0].shape[0]
    rows = count * per
    picks = member_of_row(me, rows, channels, members, group).astype(jnp.bfloat16)
    weights = softmax(s_ref[...] * scale)
    pairs = p_ref[...]
    slope = weights * (pairs - jnp.sum(weights * pairs, axis=1, keepdims=True)) * scale
    d_high, d_low = two_parts(
        spread(slope, picks) * qk_ref[...] + spread_t(slope, picks) * qkt_ref[...]
    )
    a_high, a_low = two_parts(spread_t(weights, picks) * ovt_ref[...])
    for at, width in lane_tiles(chunk):
        e = gather_tile(fields, at, width)
        c = gather_tile(grads, at, width)
        b = (
            mm(d_high, e, ((1,), (0,))) + mm(d_low, e, ((1,), (0,)))
            + mm(a_high, c, ((1,), (0,))) + mm(a_low, c, ((1,), (0,)))
        ).astype(jnp.bfloat16)
        for s in range(count):
            outs[s][:, at:at + width] = b[s * per:(s + 1) * per]


def finish_kernel(me_of, count, chunk, length, *refs):
    me = me_of()
    base, extra, out_ref = refs[:count], refs[count:2 * count], refs[-1]
    for s in range(count):
        start = chunk_start(partner(me, s), chunk, length)
        out_ref[:, pl.ds(start, chunk)] = base[s][...].astype(jnp.float32) + extra[
            s
        ][...].astype(jnp.float32)


def exchange(parts):
    count = len(parts)
    return [parts[0]] + [
        lax.ppermute(parts[s], "mem", [(i, i ^ s) for i in range(count)])
        for s in range(1, count)
    ]


def sum_over(value, name):
    size = lax.axis_size(name)
    step = 1
    while step < size:
        value = value + lax.ppermute(value, name, [(i, i ^ step) for i in range(size)])
        step *= 2
    return value


def shards(ensemble, cotangent, w_query, w_key, w_value, w_out):
    count = lax.axis_size("mem")
    group, channels, length = ensemble.shape
    members = group * count
    per = group * channels
    rows = per * count
    chunk = -(-length // (LANES * count)) * LANES
    scale = 1.0 / (length * lax.axis_size("space") * math.sqrt(channels))
    me_of = lambda: lax.axis_index("mem")
    bf, f32 = jnp.bfloat16, jnp.float32
    whole = pl.BlockSpec(memory_space=VMEM)
    anywhere = pl.BlockSpec(memory_space=pl.ANY)
    params = pltpu.CompilerParams(vmem_limit_bytes=40 * 1024 * 1024)
    part = jax.ShapeDtypeStruct((per, chunk), bf)
    square = jax.ShapeDtypeStruct((rows, rows), f32)
    pair = jax.ShapeDtypeStruct((members, members), f32)
    fields = ensemble.reshape(per, length)
    grads = cotangent.reshape(per, length)

    def cost(flops, moved):
        return pl.CostEstimate(flops=flops, bytes_accessed=moved, transcendentals=0)

    e_mine = pl.pallas_call(
        functools.partial(split_kernel, me_of, count, chunk, length),
        out_shape=[part] * count,
        in_specs=[anywhere],
        out_specs=[anywhere] * count,
        scratch_shapes=[pltpu.SemaphoreType.DMA((count,))],
        compiler_params=params,
        name="split_fields",
    )(fields)
    outcome = pl.pallas_call(
        functools.partial(split_weights_kernel, me_of, count, chunk, length, rows, channels),
        out_shape=[part] * count + [square] * 4,
        in_specs=[anywhere, anywhere] + [whole] * 4,
        out_specs=[anywhere] * count + [whole] * 4,
        scratch_shapes=[pltpu.SemaphoreType.DMA((count,))],
        compiler_params=params,
        name="split_grads",
    )(grads, e_mine[0], w_query, w_key, w_value, w_out)
    c_mine, (qk, qkt, ov, ovt) = outcome[:count], outcome[count:]

    e_cells = exchange(e_mine)
    c_cells = exchange(c_mine)

    def gram(left, right, tile, name):
        same = left is right
        operands = list(left) if same else list(left) + list(right)
        return pl.pallas_call(
            functools.partial(
                gram_kernel, me_of, count, chunk, length, group, channels, members, same
            ),
            out_shape=pair,
            in_specs=[whole] * (len(operands) + 1),
            out_specs=whole,
            compiler_params=params,
            cost_estimate=cost(2 * rows * rows * chunk, 2 * len(operands) * per * chunk),
            name=name,
        )(*operands, tile)

    scores = gram(e_cells, e_cells, qk, "score_sums")
    scores = sum_over(sum_over(scores, "space"), "mem")
    branch = pl.pallas_call(
        functools.partial(branch_kernel, me_of, count, chunk, group, channels, members, scale),
        out_shape=[part] * count,
        in_specs=[whole] * (count + 2),
        out_specs=[whole] * count,
        compiler_params=params,
        cost_estimate=cost(4 * rows * rows * chunk, 4 * rows * chunk),
        name="branch",
    )(scores, ov, *e_cells)
    branch_home = exchange(branch)

    pairs = gram(c_cells, e_cells, ov, "pair_sums")
    pairs = sum_over(sum_over(pairs, "mem"), "space")
    grad = pl.pallas_call(
        functools.partial(grad_kernel, me_of, count, chunk, group, channels, members, scale),
        out_shape=[part] * count,
        in_specs=[whole] * (2 * count + 5),
        out_specs=[whole] * count,
        compiler_params=params,
        cost_estimate=cost(8 * rows * rows * chunk, 6 * rows * chunk),
        name="input_gradient",
    )(scores, pairs, qk, qkt, ovt, *e_cells, *c_cells)
    grad_home = exchange(grad)

    def finish(base, extra, name):
        return pl.pallas_call(
            functools.partial(finish_kernel, me_of, count, chunk, length),
            out_shape=jax.ShapeDtypeStruct((per, length), f32),
            in_specs=[whole] * (2 * count),
            out_specs=whole,
            compiler_params=params,
            cost_estimate=cost(per * length, 8 * per * length),
            name=name,
        )(*base, *extra).reshape(group, channels, length)

    updated = finish(e_mine, branch_home, "updated")
    ensemble_grad = finish(c_mine, grad_home, "ensemble_grad")
    return (updated, ensemble_grad)


def solution(mesh):
    split = P("mem", None, "space")
    return jax.shard_map(
        shards,
        mesh=mesh,
        in_specs=(split, split, P(), P(), P(), P()),
        out_specs=(split, split),
        check_vma=False,
    )
```

```python
import functools
import math

import jax
import jax.numpy as jnp
from jax import lax
from jax.experimental import pallas as pl
from jax.experimental.pallas import tpu as pltpu
from jax.sharding import PartitionSpec as P

LANES = 128
HIGH = lax.Precision.HIGHEST
VMEM = pltpu.MemorySpace.VMEM


def mm(a, b, dims, precision=None):
    return lax.dot_general(
        a, b, (dims, ((), ())), precision=precision, preferred_element_type=jnp.float32
    )


def chunk_start(index, chunk, length):
    return pl.multiple_of(jnp.minimum(index * chunk, length - chunk), LANES)


def partner(me, step):
    return me ^ step


def lane_tiles(width, step=512):
    return [(at, min(step, width - at)) for at in range(0, width, step)]


def half_of(chunk):
    return -(-chunk // (2 * LANES)) * LANES


def whole_pieces(count, chunk):
    return [(s, 0, chunk) for s in range(count)]


def last_cut(count, chunk):
    pieces = whole_pieces(count, chunk)
    half = half_of(chunk)
    return pieces[:-1] + [(count - 1, 0, half), (count - 1, half, chunk - half)]


def store_pieces(outs, pieces, value, at, width, per):
    for out, (s, low, size) in zip(outs, pieces):
        a, b = max(at, low), min(at + width, low + size)
        if a < b:
            out[:, a - low:b - low] = value[s * per:(s + 1) * per, a - at:b - at]


def member_of_row(me, rows, channels, members, group):
    row = lax.broadcasted_iota(jnp.int32, (rows, members), 0)
    col = lax.broadcasted_iota(jnp.int32, (rows, members), 1)
    per_group = group * channels
    owner = (row // per_group) ^ me
    member = owner * group + (row % per_group) // channels
    return (member == col).astype(jnp.float32)


def split_kernel(me_of, count, chunk, length, x_ref, *rest):
    outs, sem = rest[-count - 1:-1], rest[-1]
    me = me_of()
    copies = [
        pltpu.make_async_copy(
            x_ref.at[:, pl.ds(chunk_start(partner(me, s), chunk, length), chunk)],
            outs[s],
            sem.at[s],
        )
        for s in range(count)
    ]
    for copy in copies:
        copy.start()
    for copy in copies:
        copy.wait()


def tiled(small, rows, channels):
    tall = jnp.concatenate([small] * (rows // channels), axis=0)
    col = lax.broadcasted_iota(jnp.int32, (channels, rows), 1)
    row = lax.broadcasted_iota(jnp.int32, (channels, rows), 0)
    spread = (col % channels == row).astype(jnp.float32)
    return mm(tall, spread, ((1,), (0,)), HIGH)


def tiles_kernel(rows, channels, wq_ref, wk_ref, wv_ref, wo_ref, qk_ref, qkt_ref, ov_ref, ovt_ref):
    wq, wk = wq_ref[...].astype(jnp.float32), wk_ref[...].astype(jnp.float32)
    wv, wo = wv_ref[...].astype(jnp.float32), wo_ref[...].astype(jnp.float32)
    wqt, wkt, wvt, wot = wq.T, wk.T, wv.T, wo.T
    qk_ref[...] = tiled(mm(wqt, wk, ((1,), (0,)), HIGH), rows, channels)
    qkt_ref[...] = tiled(mm(wkt, wq, ((1,), (0,)), HIGH), rows, channels)
    ov_ref[...] = tiled(mm(wo, wv, ((1,), (0,)), HIGH), rows, channels)
    ovt_ref[...] = tiled(mm(wvt, wot, ((1,), (0,)), HIGH), rows, channels)


def gather_tile(refs, at, width):
    return jnp.concatenate([r[:, at:at + width] for r in refs], axis=0)


def fold(weighted, picks):
    half = mm(weighted, picks, ((1,), (0,)), HIGH)
    return mm(picks, half, ((0,), (0,)), HIGH)


def masked_gram(me, count, chunk, length, left, right):
    rows = count * right[0].shape[0]
    skip = me * chunk - chunk_start(me, chunk, length)
    total = jnp.zeros((rows, rows), jnp.float32)
    for at, width in lane_tiles(chunk):
        b = gather_tile(right, at, width)
        a = b if left is right else gather_tile(left, at, width)
        lane = lax.broadcasted_iota(jnp.int32, (rows, width), 1) + at
        a = jnp.where(lane >= skip, a.astype(jnp.float32), 0.0).astype(jnp.bfloat16)
        total = total + mm(a, b, ((1,), (1,)))
    return total


def score_kernel(me_of, count, chunk, length, group, channels, members, tile_ref, *refs):
    me = me_of()
    fields, out_ref = refs[:count], refs[-1]
    rows = count * fields[0].shape[0]
    total = masked_gram(me, count, chunk, length, fields, fields)
    picks = member_of_row(me, rows, channels, members, group)
    out_ref[...] = fold(total * tile_ref[...], picks)


def pair_kernel(me_of, count, chunk, length, group, channels, members, tile_ref, s_ref, *refs):
    me = me_of()
    fields, grads, out_ref = refs[:count], refs[count:2 * count], refs[-1]
    rows = count * fields[0].shape[0]
    total = masked_gram(me, count, chunk, length, grads, fields)
    picks = member_of_row(me, rows, channels, members, group)
    out_ref[:members, :] = s_ref[...]
    out_ref[members:, :] = fold(total * tile_ref[...], picks)


def softmax(scores):
    peak = jnp.max(scores, axis=1, keepdims=True)
    exponent = jnp.exp(scores - peak)
    return exponent / jnp.sum(exponent, axis=1, keepdims=True)


def spread(small, picks):
    tall = mm(picks, small.astype(jnp.bfloat16), ((1,), (0,))).astype(jnp.bfloat16)
    return mm(tall, picks, ((1,), (1,)))


def spread_t(small, picks):
    tall = mm(picks, small.astype(jnp.bfloat16), ((1,), (1,))).astype(jnp.bfloat16)
    return mm(tall, picks, ((1,), (1,)))


def two_parts(value):
    high = value.astype(jnp.bfloat16)
    return high, (value - high.astype(jnp.float32)).astype(jnp.bfloat16)


def branch_kernel(
    me_of, count, chunk, group, channels, members, scale, pieces, ov_ref, *refs
):
    me = me_of()
    sums, fields = refs[:count], refs[count:2 * count]
    total_ref, outs = refs[2 * count], refs[2 * count + 1:]
    per = fields[0].shape[0]
    rows = count * per
    total = sums[0][...]
    for other in sums[1:]:
        total = total + other[...]
    total_ref[...] = total
    picks = member_of_row(me, rows, channels, members, group).astype(jnp.bfloat16)
    weights = softmax(total[:members, :] * scale)
    high, low = two_parts(spread(weights, picks) * ov_ref[...])
    for at, width in lane_tiles(chunk):
        e = gather_tile(fields, at, width)
        b = (mm(high, e, ((1,), (0,))) + mm(low, e, ((1,), (0,)))).astype(jnp.bfloat16)
        store_pieces(outs, pieces, b, at, width, per)


def grad_kernel(
    me_of, count, chunk, group, channels, members, scale, low, size, waits,
    s_ref, p_ref, qk_ref, qkt_ref, ovt_ref, *refs,
):
    me = me_of()
    fields, grads, outs = refs[:count], refs[count:2 * count], refs[2 * count + waits:]
    per = fields[0].shape[0]
    rows = count * per
    picks = member_of_row(me, rows, channels, members, group).astype(jnp.bfloat16)
    weights = softmax(s_ref[:members, :] * scale)
    pairs = p_ref[members:, :]
    slope = weights * (pairs - jnp.sum(weights * pairs, axis=1, keepdims=True)) * scale
    d_high, d_low = two_parts(
        spread(slope, picks) * qk_ref[...] + spread_t(slope, picks) * qkt_ref[...]
    )
    a_high, a_low = two_parts(spread_t(weights, picks) * ovt_ref[...])
    for at, width in lane_tiles(size):
        e = gather_tile(fields, low + at, width)
        c = gather_tile(grads, low + at, width)
        b = (
            mm(d_high, e, ((1,), (0,))) + mm(d_low, e, ((1,), (0,)))
            + mm(a_high, c, ((1,), (0,))) + mm(a_low, c, ((1,), (0,)))
        ).astype(jnp.bfloat16)
        for s in range(count):
            outs[s][:, at:at + width] = b[s * per:(s + 1) * per]


def finish_kernel(me_of, count, chunk, length, pieces, dep_ref, *refs):
    me = me_of()
    base, extra = refs[:count], refs[count:count + len(pieces)]
    out_ref, held, sem = refs[count + len(pieces):]
    per = base[0].shape[0]
    rows = 16
    copies = []
    for at in range(0, per, rows):
        for more, (s, low, size) in zip(extra, pieces):
            start = chunk_start(partner(me, s), chunk, length) + low
            held[at:at + rows, pl.ds(pl.multiple_of(start, LANES), size)] = base[s][
                at:at + rows, low:low + size
            ].astype(jnp.float32) + more[at:at + rows, :].astype(jnp.float32)
        copy = pltpu.make_async_copy(
            held.at[at:at + rows], out_ref.at[at:at + rows], sem.at[at // rows]
        )
        copy.start()
        copies.append(copy)
    for copy in copies:
        copy.wait()


def swap(value, step, count):
    return lax.ppermute(value, "mem", [(i, i ^ step) for i in range(count)])


def exchange(parts, pieces, count):
    return [
        part if s == 0 else swap(part, s, count) for part, (s, _, _) in zip(parts, pieces)
    ]


def sum_steps(value, name, steps):
    size = lax.axis_size(name)
    for step in steps:
        value = value + lax.ppermute(value, name, [(i, i ^ step) for i in range(size)])
    return value


def doubling(size):
    steps, step = [], 1
    while step < size:
        steps.append(step)
        step *= 2
    return steps


def shards(ensemble, cotangent, w_query, w_key, w_value, w_out):
    count = lax.axis_size("mem")
    group, channels, length = ensemble.shape
    members = group * count
    per = group * channels
    rows = per * count
    chunk = -(-length // (LANES * count)) * LANES
    scale = 1.0 / (length * lax.axis_size("space") * math.sqrt(channels))
    me_of = lambda: lax.axis_index("mem")
    bf, f32 = jnp.bfloat16, jnp.float32
    whole = pl.BlockSpec(memory_space=VMEM)
    anywhere = pl.BlockSpec(memory_space=pl.ANY)
    in_hbm = pl.BlockSpec(memory_space=pltpu.MemorySpace.HBM)
    params = pltpu.CompilerParams(vmem_limit_bytes=40 * 1024 * 1024)
    part = jax.ShapeDtypeStruct((per, chunk), bf)
    square = jax.ShapeDtypeStruct((rows, rows), f32)
    pair = jax.ShapeDtypeStruct((members, members), f32)
    fields = ensemble.reshape(per, length)
    grads = cotangent.reshape(per, length)

    def cost(flops, moved):
        return pl.CostEstimate(flops=flops, bytes_accessed=moved, transcendentals=0)

    first = min(1, count - 1)
    plain = whole_pieces(count, chunk)
    cut = last_cut(count, chunk)

    def shapes(pieces):
        return [jax.ShapeDtypeStruct((per, size), bf) for _, _, size in pieces]

    def split(operands, name):
        return pl.pallas_call(
            functools.partial(split_kernel, me_of, count, chunk, length),
            out_shape=[part] * count,
            in_specs=[anywhere] * len(operands),
            out_specs=[anywhere] * count,
            scratch_shapes=[pltpu.SemaphoreType.DMA((count,))],
            compiler_params=params,
            name=name,
        )(*operands)

    e_mine = split([fields], "split_fields")
    e_cells = exchange(e_mine, plain, count)
    qk, qkt, ov, ovt = pl.pallas_call(
        functools.partial(tiles_kernel, rows, channels),
        out_shape=[square] * 4,
        in_specs=[whole] * 4,
        out_specs=[whole] * 4,
        compiler_params=params,
        cost_estimate=cost(10**8, 4 * 4 * rows * rows),
        name="weight_tiles",
    )(w_query, w_key, w_value, w_out)
    c_mine = split([grads, e_cells[first], qk], "split_grads")
    c_cells = exchange(c_mine, plain, count)
    space_steps = doubling(lax.axis_size("space"))

    scores = pl.pallas_call(
        functools.partial(
            score_kernel, me_of, count, chunk, length, group, channels, members
        ),
        out_shape=pair,
        in_specs=[whole] * (count + 1),
        out_specs=whole,
        compiler_params=params,
        cost_estimate=cost(2 * rows * rows * chunk, 2 * rows * chunk),
        name="score_sums",
    )(qk, *e_cells)
    scores = sum_steps(scores, "space", space_steps)
    both = pl.pallas_call(
        functools.partial(
            pair_kernel, me_of, count, chunk, length, group, channels, members
        ),
        out_shape=jax.ShapeDtypeStruct((2 * members, members), f32),
        in_specs=[whole] * (2 * count + 2),
        out_specs=whole,
        compiler_params=params,
        cost_estimate=cost(2 * rows * rows * chunk, 4 * rows * chunk),
        name="pair_sums",
    )(ov, scores, *e_cells, *c_cells)
    order = sorted(range(1, count), key=lambda s: (s & (s - 1) != 0, -s))
    sums = [both] + [swap(both, s, count) for s in order]

    outcome = pl.pallas_call(
        functools.partial(
            branch_kernel, me_of, count, chunk, group, channels, members, scale, cut
        ),
        out_shape=[jax.ShapeDtypeStruct((2 * members, members), f32)] + shapes(cut),
        in_specs=[whole] * (2 * count + 1),
        out_specs=[whole] * (len(cut) + 1),
        compiler_params=params,
        cost_estimate=cost(4 * rows * rows * chunk, 4 * rows * chunk),
        name="branch",
    )(ov, *sums, *e_cells)
    mem_sums, branch = outcome[0], outcome[1:]
    pairs = sum_steps(mem_sums, "space", space_steps)
    branch_home = exchange(branch, cut, count)

    def gradient(low, size, awaited, name):
        parts = pl.pallas_call(
            functools.partial(
                grad_kernel, me_of, count, chunk, group, channels, members, scale, low,
                size, len(awaited),
            ),
            out_shape=[jax.ShapeDtypeStruct((per, size), bf)] * count,
            in_specs=[whole] * (2 * count + 5) + [anywhere] * len(awaited),
            out_specs=[whole] * count,
            compiler_params=params,
            cost_estimate=cost(8 * rows * rows * size, 6 * rows * size),
            name=name,
        )(mem_sums, pairs, qk, qkt, ovt, *e_cells, *c_cells, *awaited)
        pieces = [(s, low, size) for s in range(count)]
        return pieces, exchange(parts, pieces, count)

    half = half_of(chunk)
    pieces_a, grad_a = gradient(0, half, branch_home[1:-1], "input_gradient_a")
    pieces_b, grad_b = gradient(half, chunk - half, branch_home[-1:], "input_gradient_b")

    def finish(base, extra, pieces, after, name):
        return pl.pallas_call(
            functools.partial(finish_kernel, me_of, count, chunk, length, pieces),
            out_shape=jax.ShapeDtypeStruct((per, length), f32),
            in_specs=[anywhere] + [whole] * (count + len(pieces)),
            out_specs=in_hbm,
            scratch_shapes=[
                pltpu.VMEM((per, length), f32),
                pltpu.SemaphoreType.DMA((per // 16,)),
            ],
            compiler_params=params,
            cost_estimate=cost(per * length, 8 * per * length),
            name=name,
        )(after, *base, *extra).reshape(group, channels, length)

    updated = finish(e_mine, branch_home, cut, grad_a[first], "updated")
    ensemble_grad = finish(
        c_mine, grad_a + grad_b, pieces_a + pieces_b, grad_a[0], "ensemble_grad"
    )
    return (updated, ensemble_grad)


def solution(mesh):
    split = P("mem", None, "space")
    return jax.shard_map(
        shards,
        mesh=mesh,
        in_specs=(split, split, P(), P(), P(), P()),
        out_specs=(split, split),
        check_vma=False,
    )
```

```python
import functools
import math

import jax
import jax.numpy as jnp
from jax import lax
from jax.experimental import pallas as pl
from jax.experimental.pallas import tpu as pltpu
from jax.sharding import PartitionSpec as P

LANES = 128
HIGH = lax.Precision.HIGHEST
VMEM = pltpu.MemorySpace.VMEM


def mm(a, b, dims, precision=None):
    return lax.dot_general(
        a, b, (dims, ((), ())), precision=precision, preferred_element_type=jnp.float32
    )


def chunk_start(index, chunk, length):
    return pl.multiple_of(jnp.minimum(index * chunk, length - chunk), LANES)


def partner(me, step):
    return me ^ step


def lane_tiles(width, step=512):
    return [(at, min(step, width - at)) for at in range(0, width, step)]


def half_of(chunk):
    return -(-chunk // (2 * LANES)) * LANES


def member_of_row(me, rows, channels, members, group):
    row = lax.broadcasted_iota(jnp.int32, (rows, members), 0)
    col = lax.broadcasted_iota(jnp.int32, (rows, members), 1)
    per_group = group * channels
    owner = (row // per_group) ^ me
    member = owner * group + (row % per_group) // channels
    return (member == col).astype(jnp.float32)


def split_kernel(me_of, count, chunk, length, x_ref, *rest):
    outs, sem = rest[-count - 1:-1], rest[-1]
    me = me_of()
    copies = [
        pltpu.make_async_copy(
            x_ref.at[:, pl.ds(chunk_start(partner(me, s), chunk, length), chunk)],
            outs[s],
            sem.at[s],
        )
        for s in range(count)
    ]
    for copy in copies:
        copy.start()
    for copy in copies:
        copy.wait()


def tiled(small, rows, channels):
    tall = jnp.concatenate([small] * (rows // channels), axis=0)
    col = lax.broadcasted_iota(jnp.int32, (channels, rows), 1)
    row = lax.broadcasted_iota(jnp.int32, (channels, rows), 0)
    spread = (col % channels == row).astype(jnp.float32)
    return mm(tall, spread, ((1,), (0,)), HIGH)


def tiles_kernel(rows, channels, wq_ref, wk_ref, wv_ref, wo_ref, qk_ref, qkt_ref, ov_ref, ovt_ref):
    wq, wk = wq_ref[...].astype(jnp.float32), wk_ref[...].astype(jnp.float32)
    wv, wo = wv_ref[...].astype(jnp.float32), wo_ref[...].astype(jnp.float32)
    wqt, wkt, wvt, wot = wq.T, wk.T, wv.T, wo.T
    qk_ref[...] = tiled(mm(wqt, wk, ((1,), (0,)), HIGH), rows, channels)
    qkt_ref[...] = tiled(mm(wkt, wq, ((1,), (0,)), HIGH), rows, channels)
    ov_ref[...] = tiled(mm(wo, wv, ((1,), (0,)), HIGH), rows, channels)
    ovt_ref[...] = tiled(mm(wvt, wot, ((1,), (0,)), HIGH), rows, channels)


def gather_tile(refs, at, width):
    return jnp.concatenate([r[:, at:at + width] for r in refs], axis=0)


def fold(weighted, picks):
    half = mm(weighted, picks, ((1,), (0,)), HIGH)
    return mm(picks, half, ((0,), (0,)), HIGH)


def masked_gram(me, count, chunk, length, left, right):
    rows = count * right[0].shape[0]
    skip = me * chunk - chunk_start(me, chunk, length)
    most = max(0, count * chunk - length)
    total = jnp.zeros((rows, rows), jnp.float32)
    for at, width in lane_tiles(chunk):
        b = gather_tile(right, at, width)
        a = b if left is right else gather_tile(left, at, width)
        if at < most:
            lane = lax.broadcasted_iota(jnp.int32, (rows, width), 1) + at
            a = jnp.where(lane >= skip, a.astype(jnp.float32), 0.0).astype(jnp.bfloat16)
        total = total + mm(a, b, ((1,), (1,)))
    return total


def score_kernel(me_of, count, chunk, length, group, channels, members, tile_ref, *refs):
    me = me_of()
    fields, out_ref = refs[:count], refs[-1]
    rows = count * fields[0].shape[0]
    total = masked_gram(me, count, chunk, length, fields, fields)
    picks = member_of_row(me, rows, channels, members, group)
    out_ref[...] = fold(total * tile_ref[...], picks)


def pair_kernel(me_of, count, chunk, length, group, channels, members, tile_ref, *refs):
    me = me_of()
    fields, grads, out_ref = refs[:count], refs[count:2 * count], refs[-1]
    rows = count * fields[0].shape[0]
    total = masked_gram(me, count, chunk, length, grads, fields)
    picks = member_of_row(me, rows, channels, members, group)
    out_ref[...] = fold(total * tile_ref[...], picks)


def add_up(refs):
    return functools.reduce(jnp.add, [r[...] for r in refs])


def join_kernel(a_ref, b_ref, *refs):
    refs[-1][...] = a_ref[...] + b_ref[...]


def softmax(scores):
    peak = jnp.max(scores, axis=1, keepdims=True)
    exponent = jnp.exp(scores - peak)
    return exponent / jnp.sum(exponent, axis=1, keepdims=True)


def spread(small, picks):
    tall = mm(picks, small.astype(jnp.bfloat16), ((1,), (0,))).astype(jnp.bfloat16)
    return mm(tall, picks, ((1,), (1,)))


def spread_t(small, picks):
    tall = mm(picks, small.astype(jnp.bfloat16), ((1,), (1,))).astype(jnp.bfloat16)
    return mm(tall, picks, ((1,), (1,)))


def two_parts(value):
    high = value.astype(jnp.bfloat16)
    return high, (value - high.astype(jnp.float32)).astype(jnp.bfloat16)


def branch_kernel(
    me_of, count, chunk, group, channels, members, scale, waits, ov_ref, *refs
):
    me = me_of()
    sums, fields = refs[:count], refs[count:2 * count]
    total_ref, outs = refs[2 * count + waits], refs[2 * count + waits + 1:]
    per = fields[0].shape[0]
    rows = count * per
    total = add_up(sums)
    total_ref[...] = total
    picks = member_of_row(me, rows, channels, members, group).astype(jnp.bfloat16)
    weights = softmax(total * scale)
    high, low = two_parts(spread(weights, picks) * ov_ref[...])
    for at, width in lane_tiles(chunk):
        e = gather_tile(fields, at, width)
        b = (mm(high, e, ((1,), (0,))) + mm(low, e, ((1,), (0,)))).astype(jnp.bfloat16)
        for s in range(count):
            outs[s][:, at:at + width] = b[s * per:(s + 1) * per]


def grad_kernel(
    me_of, count, chunk, group, channels, members, scale, low, size, waits,
    s_ref, qk_ref, qkt_ref, ovt_ref, *refs,
):
    me = me_of()
    fields, grads, sums = refs[:count], refs[count:2 * count], refs[2 * count:3 * count]
    outs = refs[3 * count + waits:]
    per = fields[0].shape[0]
    rows = count * per
    picks = member_of_row(me, rows, channels, members, group).astype(jnp.bfloat16)
    weights = softmax(s_ref[...] * scale)
    pairs = add_up(sums)
    slope = weights * (pairs - jnp.sum(weights * pairs, axis=1, keepdims=True)) * scale
    d_high, d_low = two_parts(
        spread(slope, picks) * qk_ref[...] + spread_t(slope, picks) * qkt_ref[...]
    )
    a_high, a_low = two_parts(spread_t(weights, picks) * ovt_ref[...])
    for at, width in lane_tiles(size):
        e = gather_tile(fields, low + at, width)
        c = gather_tile(grads, low + at, width)
        b = (
            mm(d_high, e, ((1,), (0,))) + mm(d_low, e, ((1,), (0,)))
            + mm(a_high, c, ((1,), (0,))) + mm(a_low, c, ((1,), (0,)))
        ).astype(jnp.bfloat16)
        for s in range(count):
            outs[s][:, at:at + width] = b[s * per:(s + 1) * per]


def finish_kernel(me_of, count, chunk, length, stages, serial, waits, extras, *refs):
    me = me_of()
    base, extra = refs[waits:waits + count], refs[waits + count:waits + count + extras]
    out_ref, held, sem = refs[waits + count + extras:]
    slot = 0
    for stage in stages:
        copies = []
        for s, low, size, index, start in stage:
            held[slot, :, :size] = base[s][:, low:low + size].astype(jnp.float32) + extra[
                index
            ][:, start:start + size].astype(jnp.float32)
            place = pl.multiple_of(chunk_start(partner(me, s), chunk, length) + low, LANES)
            copy = pltpu.make_async_copy(
                held.at[slot, :, pl.ds(0, size)], out_ref.at[:, pl.ds(place, size)], sem.at[slot]
            )
            copy.start()
            if serial:
                copy.wait()
            copies.append(copy)
            slot += 1
        if not serial:
            for copy in copies:
                copy.wait()


def swap(value, step, count):
    return lax.ppermute(value, "mem", [(i, i ^ step) for i in range(count)])


def exchange(parts):
    count = len(parts)
    return [part if s == 0 else swap(part, s, count) for s, part in enumerate(parts)]


def sum_steps(value, name, steps):
    size = lax.axis_size(name)
    for step in steps:
        value = value + lax.ppermute(value, name, [(i, i ^ step) for i in range(size)])
    return value


def doubling(size):
    steps, step = [], 1
    while step < size:
        steps.append(step)
        step *= 2
    return steps


def shards(ensemble, cotangent, w_query, w_key, w_value, w_out):
    count = lax.axis_size("mem")
    group, channels, length = ensemble.shape
    members = group * count
    per = group * channels
    rows = per * count
    chunk = -(-length // (LANES * count)) * LANES
    scale = 1.0 / (length * lax.axis_size("space") * math.sqrt(channels))
    me_of = lambda: lax.axis_index("mem")
    bf, f32 = jnp.bfloat16, jnp.float32
    whole = pl.BlockSpec(memory_space=VMEM)
    anywhere = pl.BlockSpec(memory_space=pl.ANY)
    in_hbm = pl.BlockSpec(memory_space=pltpu.MemorySpace.HBM)
    params = pltpu.CompilerParams(vmem_limit_bytes=16 * 1024 * 1024 + 24 * rows * rows)
    part = jax.ShapeDtypeStruct((per, chunk), bf)
    square = jax.ShapeDtypeStruct((rows, rows), f32)
    pair = jax.ShapeDtypeStruct((members, members), f32)
    fields = ensemble.reshape(per, length)
    grads = cotangent.reshape(per, length)

    def cost(flops, moved):
        return pl.CostEstimate(flops=flops, bytes_accessed=moved, transcendentals=0)

    first = min(1, count - 1)

    def split(operands, name):
        return pl.pallas_call(
            functools.partial(split_kernel, me_of, count, chunk, length),
            out_shape=[part] * count,
            in_specs=[anywhere] * len(operands),
            out_specs=[anywhere] * count,
            scratch_shapes=[pltpu.SemaphoreType.DMA((count,))],
            compiler_params=params,
            name=name,
        )(*operands)

    e_mine = split([fields], "split_fields")
    e_cells = exchange(e_mine)
    qk, qkt, ov, ovt = pl.pallas_call(
        functools.partial(tiles_kernel, rows, channels),
        out_shape=[square] * 4,
        in_specs=[whole] * 4,
        out_specs=[whole] * 4,
        compiler_params=params,
        cost_estimate=cost(10**8, 4 * 4 * rows * rows),
        name="weight_tiles",
    )(w_query, w_key, w_value, w_out)
    c_mine = split([grads, e_cells[first], qk], "split_grads")
    c_cells = exchange(c_mine)
    space_steps = doubling(lax.axis_size("space"))

    def join(value, name, step, waited):
        size = lax.axis_size(name)
        other = lax.ppermute(value, name, [(i, i ^ step) for i in range(size)])
        return pl.pallas_call(
            join_kernel,
            out_shape=pair,
            in_specs=[whole] * 2 + [anywhere] * len(waited),
            out_specs=whole,
            compiler_params=params,
            cost_estimate=cost(members * members, 12 * members * members),
            name="join_sums",
        )(value, other, *waited)

    scores = pl.pallas_call(
        functools.partial(
            score_kernel, me_of, count, chunk, length, group, channels, members
        ),
        out_shape=pair,
        in_specs=[whole] * (count + 1),
        out_specs=whole,
        compiler_params=params,
        cost_estimate=cost(2 * rows * rows * chunk, 2 * rows * chunk),
        name="score_sums",
    )(qk, *e_cells)
    scores = sum_steps(scores, "space", space_steps[:-1])
    scores = join(scores, "space", space_steps[-1], c_cells[first:first + 1])
    order = sorted(range(1, count), key=lambda s: (s & (s - 1) != 0, -s))
    score_parts = [scores] + [swap(scores, s, count) for s in order]
    waited = score_parts[:1]
    pairs = pl.pallas_call(
        functools.partial(
            pair_kernel, me_of, count, chunk, length, group, channels, members
        ),
        out_shape=pair,
        in_specs=[whole] * (2 * count + 1) + [anywhere] * len(waited),
        out_specs=whole,
        compiler_params=params,
        cost_estimate=cost(2 * rows * rows * chunk, 4 * rows * chunk),
        name="pair_sums",
    )(ov, *e_cells, *c_cells, *waited)
    ahead = [pairs]
    outcome = pl.pallas_call(
        functools.partial(
            branch_kernel, me_of, count, chunk, group, channels, members, scale, len(ahead),
        ),
        out_shape=[pair] + [part] * count,
        in_specs=[whole] * (2 * count + 1) + [anywhere] * len(ahead),
        out_specs=[whole] * (count + 1),
        compiler_params=params,
        cost_estimate=cost(4 * rows * rows * chunk, 4 * rows * chunk),
        name="branch",
    )(ov, *score_parts, *e_cells, *ahead)
    scores, branch = outcome[0], outcome[1:]
    branch_home = exchange(branch)
    pairs = sum_steps(pairs, "space", space_steps[:-1])
    pairs = join(pairs, "space", space_steps[-1], branch_home[first:first + 1])
    pair_parts = [pairs] + [swap(pairs, s, count) for s in order]

    def gradient(low, size, awaited, name):
        parts = pl.pallas_call(
            functools.partial(
                grad_kernel, me_of, count, chunk, group, channels, members, scale, low,
                size, len(awaited),
            ),
            out_shape=[jax.ShapeDtypeStruct((per, size), bf)] * count,
            in_specs=[whole] * (3 * count + 4) + [anywhere] * len(awaited),
            out_specs=[whole] * count,
            compiler_params=params,
            cost_estimate=cost(8 * rows * rows * size, 6 * rows * size),
            name=name,
        )(scores, qk, qkt, ovt, *e_cells, *c_cells, *pair_parts, *awaited)
        return exchange(parts)

    half = half_of(chunk)
    grad_a = gradient(0, half, branch_home[1:], "input_gradient_a")
    grad_b = gradient(half, chunk - half, branch_home[1:], "input_gradient_b")

    rest = chunk - half
    serial = count * chunk - length > rest

    def finish(base, extra, stages, before, after, name):
        slots = sum(len(stage) for stage in stages)
        waited = list(before) + list(after)
        return pl.pallas_call(
            functools.partial(
                finish_kernel, me_of, count, chunk, length, stages, serial, len(waited),
                len(extra),
            ),
            out_shape=jax.ShapeDtypeStruct((per, length), f32),
            in_specs=[anywhere] * len(waited) + [whole] * (count + len(extra)),
            out_specs=in_hbm,
            scratch_shapes=[
                pltpu.VMEM((slots, per, half), f32),
                pltpu.SemaphoreType.DMA((slots,)),
            ],
            input_output_aliases={0: 0} if before else {},
            compiler_params=params,
            cost_estimate=cost(per * length, 8 * per * length),
            name=name,
        )(*waited, *base, *extra)

    steps = list(range(count))
    updated = finish(
        e_mine, branch_home,
        [[(s, 0, half, s, 0) for s in steps], [(s, half, rest, s, half) for s in steps]],
        [], [grad_a[first]], "updated",
    )
    ensemble_grad = finish(
        c_mine, grad_a + grad_b[:1],
        [[(s, 0, half, s, 0) for s in steps], [(0, half, rest, count, 0)]],
        [], [], "ensemble_grad_early",
    )
    if count > 1:
        ensemble_grad = finish(
            c_mine, grad_b[1:], [[(s, half, rest, s - 1, 0) for s in steps[1:]]],
            [ensemble_grad], [], "ensemble_grad_late",
        )
    shape = (group, channels, length)
    return (updated.reshape(shape), ensemble_grad.reshape(shape))


def solution(mesh):
    split = P("mem", None, "space")
    return jax.shard_map(
        shards,
        mesh=mesh,
        in_specs=(split, split, P(), P(), P(), P()),
        out_specs=(split, split),
        check_vma=False,
    )
```

```python
import functools
import math

import jax
import jax.numpy as jnp
from jax import lax
from jax.experimental import pallas as pl
from jax.experimental.pallas import tpu as pltpu
from jax.sharding import PartitionSpec as P

LANES = 128
HIGH = lax.Precision.HIGHEST
VMEM = pltpu.MemorySpace.VMEM


def mm(a, b, dims, precision=None):
    return lax.dot_general(
        a, b, (dims, ((), ())), precision=precision, preferred_element_type=jnp.float32
    )


def chunk_start(index, chunk, length):
    return pl.multiple_of(jnp.minimum(index * chunk, length - chunk), LANES)


def partner(me, step):
    return me ^ step


def lane_tiles(width, step=512):
    return [(at, min(step, width - at)) for at in range(0, width, step)]


def half_of(chunk):
    return -(-chunk // (2 * LANES)) * LANES


def member_of_row(me, rows, channels, members, group):
    row = lax.broadcasted_iota(jnp.int32, (rows, members), 0)
    col = lax.broadcasted_iota(jnp.int32, (rows, members), 1)
    per_group = group * channels
    owner = (row // per_group) ^ me
    member = owner * group + (row % per_group) // channels
    return (member == col).astype(jnp.float32)


def split_kernel(me_of, count, chunk, length, x_ref, *rest):
    outs, sem = rest[-count - 1:-1], rest[-1]
    me = me_of()
    copies = [
        pltpu.make_async_copy(
            x_ref.at[:, pl.ds(chunk_start(partner(me, s), chunk, length), chunk)],
            outs[s],
            sem.at[s],
        )
        for s in range(count)
    ]
    for copy in copies:
        copy.start()
    for copy in copies:
        copy.wait()


def tiled(small, rows, channels):
    tall = jnp.concatenate([small] * (rows // channels), axis=0)
    col = lax.broadcasted_iota(jnp.int32, (channels, rows), 1)
    row = lax.broadcasted_iota(jnp.int32, (channels, rows), 0)
    spread = (col % channels == row).astype(jnp.float32)
    return mm(tall, spread, ((1,), (0,)), HIGH)


def tiles_kernel(rows, channels, wq_ref, wk_ref, wv_ref, wo_ref, qk_ref, qkt_ref, ov_ref, ovt_ref):
    wq, wk = wq_ref[...].astype(jnp.float32), wk_ref[...].astype(jnp.float32)
    wv, wo = wv_ref[...].astype(jnp.float32), wo_ref[...].astype(jnp.float32)
    wqt, wkt, wvt, wot = wq.T, wk.T, wv.T, wo.T
    qk_ref[...] = tiled(mm(wqt, wk, ((1,), (0,)), HIGH), rows, channels)
    qkt_ref[...] = tiled(mm(wkt, wq, ((1,), (0,)), HIGH), rows, channels)
    ov_ref[...] = tiled(mm(wo, wv, ((1,), (0,)), HIGH), rows, channels)
    ovt_ref[...] = tiled(mm(wvt, wot, ((1,), (0,)), HIGH), rows, channels)


def gather_tile(refs, at, width):
    return jnp.concatenate([r[:, at:at + width] for r in refs], axis=0)


def three_parts(value):
    parts = []
    for _ in range(3):
        parts.append(value.astype(jnp.bfloat16))
        value = value - parts[-1].astype(jnp.float32)
    return parts


def fold(me, weighted, channels, members, group):
    rows = weighted.shape[0]
    half = jnp.sum(weighted.reshape(members, channels, rows), axis=1)
    picks = member_of_row(me, rows, channels, members, group).astype(jnp.bfloat16)
    half = sum(mm(part, picks, ((1,), (0,))) for part in three_parts(half))
    local = lax.broadcasted_iota(jnp.int32, (members, members), 1)
    member = lax.broadcasted_iota(jnp.int32, (members, members), 0)
    order = (((local // group) ^ me) * group + local % group == member).astype(jnp.bfloat16)
    return sum(mm(order, part, ((1,), (0,))) for part in three_parts(half))


def masked_gram(me, count, chunk, length, left, right):
    rows = count * right[0].shape[0]
    skip = me * chunk - chunk_start(me, chunk, length)
    most = max(0, count * chunk - length)
    total = jnp.zeros((rows, rows), jnp.float32)
    for at, width in lane_tiles(chunk):
        b = gather_tile(right, at, width)
        a = b if left is right else gather_tile(left, at, width)
        if at < most:
            lane = lax.broadcasted_iota(jnp.int32, (rows, width), 1) + at
            a = jnp.where(lane >= skip, a.astype(jnp.float32), 0.0).astype(jnp.bfloat16)
        total = total + mm(a, b, ((1,), (1,)))
    return total


def score_kernel(me_of, count, chunk, length, group, channels, members, tile_ref, *refs):
    me = me_of()
    fields, out_ref = refs[:count], refs[-1]
    total = masked_gram(me, count, chunk, length, fields, fields)
    out_ref[...] = fold(me, total * tile_ref[...], channels, members, group)


def pair_kernel(me_of, count, chunk, length, group, channels, members, tile_ref, *refs):
    me = me_of()
    fields, grads, out_ref = refs[:count], refs[count:2 * count], refs[-1]
    total = masked_gram(me, count, chunk, length, grads, fields)
    out_ref[...] = fold(me, total * tile_ref[...], channels, members, group)


def add_up(refs):
    return functools.reduce(jnp.add, [r[...] for r in refs])


def join_kernel(a_ref, b_ref, *refs):
    refs[-1][...] = a_ref[...] + b_ref[...]


def softmax(scores):
    peak = jnp.max(scores, axis=1, keepdims=True)
    exponent = jnp.exp(scores - peak)
    return exponent / jnp.sum(exponent, axis=1, keepdims=True)


def spread(small, picks):
    tall = mm(picks, small.astype(jnp.bfloat16), ((1,), (0,))).astype(jnp.bfloat16)
    return mm(tall, picks, ((1,), (1,)))


def spread_t(small, picks):
    tall = mm(picks, small.astype(jnp.bfloat16), ((1,), (1,))).astype(jnp.bfloat16)
    return mm(tall, picks, ((1,), (1,)))


def two_parts(value):
    high = value.astype(jnp.bfloat16)
    return high, (value - high.astype(jnp.float32)).astype(jnp.bfloat16)


def branch_kernel(
    me_of, count, chunk, group, channels, members, scale, waits, ov_ref, *refs
):
    me = me_of()
    sums, fields = refs[:count], refs[count:2 * count]
    total_ref, outs = refs[2 * count + waits], refs[2 * count + waits + 1:]
    per = fields[0].shape[0]
    rows = count * per
    total = add_up(sums)
    total_ref[...] = total
    picks = member_of_row(me, rows, channels, members, group).astype(jnp.bfloat16)
    weights = softmax(total * scale)
    high, low = two_parts(spread(weights, picks) * ov_ref[...])
    for at, width in lane_tiles(chunk):
        e = gather_tile(fields, at, width)
        b = (mm(high, e, ((1,), (0,))) + mm(low, e, ((1,), (0,)))).astype(jnp.bfloat16)
        for s in range(count):
            outs[s][:, at:at + width] = b[s * per:(s + 1) * per]


def transposed_weights_kernel(
    me_of, channels, members, group, scale, s_ref, ovt_ref, w_ref, high_ref, low_ref
):
    rows = ovt_ref.shape[0]
    picks = member_of_row(me_of(), rows, channels, members, group).astype(jnp.bfloat16)
    weights = softmax(s_ref[...] * scale)
    w_ref[...] = weights
    high_ref[...], low_ref[...] = two_parts(spread_t(weights, picks) * ovt_ref[...])


def grad_kernel(
    me_of, count, chunk, group, channels, members, scale, low, size, waits,
    w_ref, qk_ref, qkt_ref, a_high_ref, a_low_ref, *refs,
):
    me = me_of()
    fields, grads, sums = refs[:count], refs[count:2 * count], refs[2 * count:3 * count]
    outs = refs[3 * count + waits:]
    per = fields[0].shape[0]
    rows = count * per
    picks = member_of_row(me, rows, channels, members, group).astype(jnp.bfloat16)
    weights = w_ref[...]
    pairs = add_up(sums)
    slope = weights * (pairs - jnp.sum(weights * pairs, axis=1, keepdims=True)) * scale
    d_high, d_low = two_parts(
        spread(slope, picks) * qk_ref[...] + spread_t(slope, picks) * qkt_ref[...]
    )
    a_high, a_low = a_high_ref[...], a_low_ref[...]
    for at, width in lane_tiles(size):
        e = gather_tile(fields, low + at, width)
        c = gather_tile(grads, low + at, width)
        b = (
            mm(d_high, e, ((1,), (0,))) + mm(d_low, e, ((1,), (0,)))
            + mm(a_high, c, ((1,), (0,))) + mm(a_low, c, ((1,), (0,)))
        ).astype(jnp.bfloat16)
        for s in range(count):
            outs[s][:, at:at + width] = b[s * per:(s + 1) * per]


def finish_kernel(me_of, count, chunk, length, stages, serial, waits, extras, *refs):
    me = me_of()
    base, extra = refs[waits:waits + count], refs[waits + count:waits + count + extras]
    out_ref, held, sem = refs[waits + count + extras:]
    slot = 0
    for stage in stages:
        copies = []
        for s, low, size, index, start in stage:
            held[slot, :, :size] = base[s][:, low:low + size].astype(jnp.float32) + extra[
                index
            ][:, start:start + size].astype(jnp.float32)
            place = pl.multiple_of(chunk_start(partner(me, s), chunk, length) + low, LANES)
            copy = pltpu.make_async_copy(
                held.at[slot, :, pl.ds(0, size)], out_ref.at[:, pl.ds(place, size)], sem.at[slot]
            )
            copy.start()
            if serial:
                copy.wait()
            copies.append(copy)
            slot += 1
        if not serial:
            for copy in copies:
                copy.wait()


def swap(value, step, count):
    return lax.ppermute(value, "mem", [(i, i ^ step) for i in range(count)])


def exchange(parts):
    count = len(parts)
    return [part if s == 0 else swap(part, s, count) for s, part in enumerate(parts)]


def sum_steps(value, name, steps):
    size = lax.axis_size(name)
    for step in steps:
        value = value + lax.ppermute(value, name, [(i, i ^ step) for i in range(size)])
    return value


def doubling(size):
    steps, step = [], 1
    while step < size:
        steps.append(step)
        step *= 2
    return steps


def shards(ensemble, cotangent, w_query, w_key, w_value, w_out):
    count = lax.axis_size("mem")
    group, channels, length = ensemble.shape
    members = group * count
    per = group * channels
    rows = per * count
    chunk = -(-length // (LANES * count)) * LANES
    scale = 1.0 / (length * lax.axis_size("space") * math.sqrt(channels))
    me_of = lambda: lax.axis_index("mem")
    bf, f32 = jnp.bfloat16, jnp.float32
    whole = pl.BlockSpec(memory_space=VMEM)
    anywhere = pl.BlockSpec(memory_space=pl.ANY)
    in_hbm = pl.BlockSpec(memory_space=pltpu.MemorySpace.HBM)
    params = pltpu.CompilerParams(vmem_limit_bytes=16 * 1024 * 1024 + 24 * rows * rows)
    part = jax.ShapeDtypeStruct((per, chunk), bf)
    square = jax.ShapeDtypeStruct((rows, rows), f32)
    pair = jax.ShapeDtypeStruct((members, members), f32)
    fields = ensemble.reshape(per, length)
    grads = cotangent.reshape(per, length)

    def cost(flops, moved):
        return pl.CostEstimate(flops=flops, bytes_accessed=moved, transcendentals=0)

    first = min(1, count - 1)

    def split(operands, name):
        return pl.pallas_call(
            functools.partial(split_kernel, me_of, count, chunk, length),
            out_shape=[part] * count,
            in_specs=[anywhere] * len(operands),
            out_specs=[anywhere] * count,
            scratch_shapes=[pltpu.SemaphoreType.DMA((count,))],
            compiler_params=params,
            name=name,
        )(*operands)

    e_mine = split([fields], "split_fields")
    e_cells = exchange(e_mine)
    qk, qkt, ov, ovt = pl.pallas_call(
        functools.partial(tiles_kernel, rows, channels),
        out_shape=[square] * 4,
        in_specs=[whole] * 4,
        out_specs=[whole] * 4,
        compiler_params=params,
        cost_estimate=cost(10**8, 4 * 4 * rows * rows),
        name="weight_tiles",
    )(w_query, w_key, w_value, w_out)
    c_mine = split([grads, e_cells[first], qk], "split_grads")
    c_cells = exchange(c_mine)
    space_steps = doubling(lax.axis_size("space"))

    def join(value, name, step, waited):
        size = lax.axis_size(name)
        other = lax.ppermute(value, name, [(i, i ^ step) for i in range(size)])
        return pl.pallas_call(
            join_kernel,
            out_shape=pair,
            in_specs=[whole] * 2 + [anywhere] * len(waited),
            out_specs=whole,
            compiler_params=params,
            cost_estimate=cost(members * members, 12 * members * members),
            name="join_sums",
        )(value, other, *waited)

    scores = pl.pallas_call(
        functools.partial(
            score_kernel, me_of, count, chunk, length, group, channels, members
        ),
        out_shape=pair,
        in_specs=[whole] * (count + 1),
        out_specs=whole,
        compiler_params=params,
        cost_estimate=cost(2 * rows * rows * chunk, 2 * rows * chunk),
        name="score_sums",
    )(qk, *e_cells)
    scores = sum_steps(scores, "space", space_steps[:-1])
    scores = join(scores, "space", space_steps[-1], c_cells[first:first + 1])
    order = sorted(range(1, count), key=lambda s: (s & (s - 1) == 0, s))
    score_parts = [scores] + [swap(scores, s, count) for s in order]
    waited = score_parts[:1]
    pairs = pl.pallas_call(
        functools.partial(
            pair_kernel, me_of, count, chunk, length, group, channels, members
        ),
        out_shape=pair,
        in_specs=[whole] * (2 * count + 1) + [anywhere] * len(waited),
        out_specs=whole,
        compiler_params=params,
        cost_estimate=cost(2 * rows * rows * chunk, 4 * rows * chunk),
        name="pair_sums",
    )(ov, *e_cells, *c_cells, *waited)
    ahead = [pairs]
    outcome = pl.pallas_call(
        functools.partial(
            branch_kernel, me_of, count, chunk, group, channels, members, scale, len(ahead),
        ),
        out_shape=[pair] + [part] * count,
        in_specs=[whole] * (2 * count + 1) + [anywhere] * len(ahead),
        out_specs=[whole] * (count + 1),
        compiler_params=params,
        cost_estimate=cost(4 * rows * rows * chunk, 4 * rows * chunk),
        name="branch",
    )(ov, *score_parts, *e_cells, *ahead)
    scores, branch = outcome[0], outcome[1:]
    branch_home = exchange(branch)
    pairs = sum_steps(pairs, "space", space_steps[:-1])
    pairs = join(pairs, "space", space_steps[-1], branch_home[first:first + 1])
    pair_parts = [pairs] + [swap(pairs, s, count) for s in order]

    weights, a_high, a_low = pl.pallas_call(
        functools.partial(
            transposed_weights_kernel, me_of, channels, members, group, scale
        ),
        out_shape=[pair] + [jax.ShapeDtypeStruct((rows, rows), bf)] * 2,
        in_specs=[whole] * 2,
        out_specs=[whole] * 3,
        compiler_params=params,
        cost_estimate=cost(10**8, 8 * rows * rows),
        name="transposed_weights",
    )(scores, ovt)

    def gradient(low, size, awaited, name):
        parts = pl.pallas_call(
            functools.partial(
                grad_kernel, me_of, count, chunk, group, channels, members, scale, low,
                size, len(awaited),
            ),
            out_shape=[jax.ShapeDtypeStruct((per, size), bf)] * count,
            in_specs=[whole] * (3 * count + 5) + [anywhere] * len(awaited),
            out_specs=[whole] * count,
            compiler_params=params,
            cost_estimate=cost(8 * rows * rows * size, 6 * rows * size),
            name=name,
        )(weights, qk, qkt, a_high, a_low, *e_cells, *c_cells, *pair_parts, *awaited)
        return exchange(parts)

    half = half_of(chunk)
    grad_a = gradient(0, half, branch_home[1:], "input_gradient_a")
    grad_b = gradient(half, chunk - half, branch_home[1:], "input_gradient_b")

    rest = chunk - half
    serial = count * chunk - length > rest

    def finish(base, extra, stages, before, after, name):
        slots = sum(len(stage) for stage in stages)
        waited = list(before) + list(after)
        return pl.pallas_call(
            functools.partial(
                finish_kernel, me_of, count, chunk, length, stages, serial, len(waited),
                len(extra),
            ),
            out_shape=jax.ShapeDtypeStruct((per, length), f32),
            in_specs=[anywhere] * len(waited) + [whole] * (count + len(extra)),
            out_specs=in_hbm,
            scratch_shapes=[
                pltpu.VMEM((slots, per, half), f32),
                pltpu.SemaphoreType.DMA((slots,)),
            ],
            input_output_aliases={0: 0} if before else {},
            compiler_params=params,
            cost_estimate=cost(per * length, 8 * per * length),
            name=name,
        )(*waited, *base, *extra)

    steps = list(range(count))
    updated = finish(
        e_mine, branch_home,
        [[(s, 0, half, s, 0) for s in steps], [(s, half, rest, s, half) for s in steps]],
        [], [grad_a[first]], "updated",
    )
    ensemble_grad = finish(
        c_mine, grad_a + grad_b[:1],
        [[(s, 0, half, s, 0) for s in steps], [(0, half, rest, count, 0)]],
        [], [], "ensemble_grad_early",
    )
    if count > 1:
        ensemble_grad = finish(
            c_mine, grad_b[1:], [[(s, half, rest, s - 1, 0) for s in steps[1:]]],
            [ensemble_grad], [], "ensemble_grad_late",
        )
    shape = (group, channels, length)
    return (updated.reshape(shape), ensemble_grad.reshape(shape))


def solution(mesh):
    split = P("mem", None, "space")
    return jax.shard_map(
        shards,
        mesh=mesh,
        in_specs=(split, split, P(), P(), P(), P()),
        out_specs=(split, split),
        check_vma=False,
    )
```

```python
import functools
import math

import jax
import jax.numpy as jnp
from jax import lax
from jax.experimental import pallas as pl
from jax.experimental.pallas import tpu as pltpu
from jax.sharding import PartitionSpec as P

LANES = 128
HIGH = lax.Precision.HIGHEST
VMEM = pltpu.MemorySpace.VMEM


def mm(a, b, dims, precision=None):
    return lax.dot_general(
        a, b, (dims, ((), ())), precision=precision, preferred_element_type=jnp.float32
    )


def chunk_start(index, chunk, length):
    return pl.multiple_of(jnp.minimum(index * chunk, length - chunk), LANES)


def partner(me, step):
    return me ^ step


def tile_layout(length, count):
    main, left = divmod(length // LANES, count)
    if left and 2 * left == count:
        return main, 1
    return main + (left > 0), 0


def tile_groups(first, last, half, most=4):
    tiles = list(range(first, last)) + [None] * half
    return [tiles[at:at + most] for at in range(0, len(tiles), most)]


def swap_halves(value):
    return pltpu.roll(value, LANES // 2, 1)


def left_half(shape):
    return lax.broadcasted_iota(jnp.int32, shape, 1) < LANES // 2


def pack(tile, odd=None):
    half = tile.shape[0] // 2
    top, low = tile[:half], tile[half:]
    left, right = top, swap_halves(low)
    if odd is not None:
        second = lax.broadcasted_iota(jnp.int32, top.shape, 1) * 0 + odd == 1
        left, right = jnp.where(second, swap_halves(top), top), jnp.where(second, low, right)
    return jnp.where(left_half(top.shape), left, right)


def tile_of(ref, tile, per, main):
    if tile is not None:
        return ref[tile * per:(tile + 1) * per, :]
    packed = ref[main * per:, :].astype(jnp.float32)
    return jnp.concatenate([packed, swap_halves(packed)], axis=0).astype(jnp.bfloat16)


def gather_tiles(refs, group, per, main):
    return jnp.concatenate(
        [
            jnp.concatenate([tile_of(ref, tile, per, main) for tile in group], axis=1)
            for ref in refs
        ],
        axis=0,
    )


def store_tiles(outs, value, group, per, first, last):
    for at, tile in enumerate(group):
        for s, out in enumerate(outs):
            rows = value[s * per:(s + 1) * per, at * LANES:(at + 1) * LANES]
            if tile is None:
                out[(last - first) * per:, :] = pack(rows).astype(jnp.bfloat16)
            else:
                out[(tile - first) * per:(tile - first + 1) * per, :] = rows.astype(
                    jnp.bfloat16
                )


def member_of_row(me, rows, channels, members, group):
    row = lax.broadcasted_iota(jnp.int32, (rows, members), 0)
    col = lax.broadcasted_iota(jnp.int32, (rows, members), 1)
    per_group = group * channels
    owner = (row // per_group) ^ me
    member = owner * group + (row % per_group) // channels
    return (member == col).astype(jnp.float32)


def split_kernel(me_of, count, main, half, length, x_ref, *rest):
    outs = rest[-count:]
    me = me_of()
    per = x_ref.shape[0]
    for s in range(count):
        owner = partner(me, s)
        start = chunk_start(owner, main * LANES, length)
        for tile in range(main):
            place = pl.multiple_of(start + tile * LANES, LANES)
            outs[s][tile * per:(tile + 1) * per, :] = x_ref[:, pl.ds(place, LANES)]
        if half:
            place = pl.multiple_of((main * count + owner // 2) * LANES, LANES)
            shared = x_ref[:, pl.ds(place, LANES)].astype(jnp.float32)
            outs[s][main * per:, :] = pack(shared, owner % 2).astype(jnp.bfloat16)


def tiled(small, rows, channels):
    tall = jnp.concatenate([small] * (rows // channels), axis=0)
    col = lax.broadcasted_iota(jnp.int32, (channels, rows), 1)
    row = lax.broadcasted_iota(jnp.int32, (channels, rows), 0)
    spread = (col % channels == row).astype(jnp.float32)
    return mm(tall, spread, ((1,), (0,)), HIGH)


def tiles_kernel(rows, channels, wq_ref, wk_ref, wv_ref, wo_ref, qk_ref, qkt_ref, ov_ref, ovt_ref):
    wq, wk = wq_ref[...].astype(jnp.float32), wk_ref[...].astype(jnp.float32)
    wv, wo = wv_ref[...].astype(jnp.float32), wo_ref[...].astype(jnp.float32)
    wqt, wkt, wvt, wot = wq.T, wk.T, wv.T, wo.T
    qk_ref[...] = tiled(mm(wqt, wk, ((1,), (0,)), HIGH), rows, channels)
    qkt_ref[...] = tiled(mm(wkt, wq, ((1,), (0,)), HIGH), rows, channels)
    ov_ref[...] = tiled(mm(wo, wv, ((1,), (0,)), HIGH), rows, channels)
    ovt_ref[...] = tiled(mm(wvt, wot, ((1,), (0,)), HIGH), rows, channels)


def three_parts(value):
    parts = []
    for _ in range(3):
        parts.append(value.astype(jnp.bfloat16))
        value = value - parts[-1].astype(jnp.float32)
    return parts


def fold(me, weighted, channels, members, group):
    rows = weighted.shape[0]
    half = jnp.sum(weighted.reshape(members, channels, rows), axis=1)
    picks = member_of_row(me, rows, channels, members, group).astype(jnp.bfloat16)
    half = sum(mm(part, picks, ((1,), (0,))) for part in three_parts(half))
    local = lax.broadcasted_iota(jnp.int32, (members, members), 1)
    member = lax.broadcasted_iota(jnp.int32, (members, members), 0)
    order = (((local // group) ^ me) * group + local % group == member).astype(jnp.bfloat16)
    return sum(mm(order, part, ((1,), (0,))) for part in three_parts(half))


def masked_gram(me, count, main, half, per, length, left, right):
    rows = count * per
    chunk = main * LANES
    skip = me * chunk - chunk_start(me, chunk, length)
    most = max(0, count * chunk - length)
    total = jnp.zeros((rows, rows), jnp.float32)
    at = 0
    for group in tile_groups(0, main, half):
        b = gather_tiles(right, group, per, main)
        a = b if left is right else gather_tiles(left, group, per, main)
        if at < most or None in group:
            lane = lax.broadcasted_iota(jnp.int32, a.shape, 1) + at
            valid = (lane >= skip) & (lane < chunk + LANES // 2)
            a = jnp.where(valid, a.astype(jnp.float32), 0.0).astype(jnp.bfloat16)
        total = total + mm(a, b, ((1,), (1,)))
        at += len(group) * LANES
    return total


def score_kernel(me_of, count, main, half, per, length, group, channels, members, tile_ref, *refs):
    me = me_of()
    fields, out_ref = refs[:count], refs[-1]
    total = masked_gram(me, count, main, half, per, length, fields, fields)
    out_ref[...] = fold(me, total * tile_ref[...], channels, members, group)


def pair_kernel(me_of, count, main, half, per, length, group, channels, members, tile_ref, *refs):
    me = me_of()
    fields, grads, out_ref = refs[:count], refs[count:2 * count], refs[-1]
    total = masked_gram(me, count, main, half, per, length, grads, fields)
    out_ref[...] = fold(me, total * tile_ref[...], channels, members, group)


def add_up(refs):
    return functools.reduce(jnp.add, [r[...] for r in refs])


def join_kernel(a_ref, b_ref, *refs):
    refs[-1][...] = a_ref[...] + b_ref[...]


def softmax(scores):
    peak = jnp.max(scores, axis=1, keepdims=True)
    exponent = jnp.exp(scores - peak)
    return exponent / jnp.sum(exponent, axis=1, keepdims=True)


def spread(small, picks):
    tall = mm(picks, small.astype(jnp.bfloat16), ((1,), (0,))).astype(jnp.bfloat16)
    return mm(tall, picks, ((1,), (1,)))


def spread_t(small, picks):
    tall = mm(picks, small.astype(jnp.bfloat16), ((1,), (1,))).astype(jnp.bfloat16)
    return mm(tall, picks, ((1,), (1,)))


def two_parts(value):
    high = value.astype(jnp.bfloat16)
    return high, (value - high.astype(jnp.float32)).astype(jnp.bfloat16)


def branch_kernel(
    me_of, count, main, half, per, group, channels, members, scale, waits, ov_ref, *refs
):
    me = me_of()
    sums, fields = refs[:count], refs[count:2 * count]
    total_ref, outs = refs[2 * count + waits], refs[2 * count + waits + 1:]
    rows = count * per
    total = add_up(sums)
    total_ref[...] = total
    picks = member_of_row(me, rows, channels, members, group).astype(jnp.bfloat16)
    weights = softmax(total * scale)
    high, low = two_parts(spread(weights, picks) * ov_ref[...])
    for tiles in tile_groups(0, main, half):
        e = gather_tiles(fields, tiles, per, main)
        value = mm(high, e, ((1,), (0,))) + mm(low, e, ((1,), (0,)))
        store_tiles(outs, value, tiles, per, 0, main)


def transposed_weights_kernel(
    me_of, channels, members, group, scale, s_ref, ovt_ref, w_ref, high_ref, low_ref
):
    rows = ovt_ref.shape[0]
    picks = member_of_row(me_of(), rows, channels, members, group).astype(jnp.bfloat16)
    weights = softmax(s_ref[...] * scale)
    w_ref[...] = weights
    high_ref[...], low_ref[...] = two_parts(spread_t(weights, picks) * ovt_ref[...])


def grad_kernel(
    me_of, count, main, half, per, group, channels, members, scale, first, last, waits,
    w_ref, qk_ref, qkt_ref, a_high_ref, a_low_ref, *refs,
):
    me = me_of()
    fields, grads, sums = refs[:count], refs[count:2 * count], refs[2 * count:3 * count]
    outs = refs[3 * count + waits:]
    rows = count * per
    picks = member_of_row(me, rows, channels, members, group).astype(jnp.bfloat16)
    weights = w_ref[...]
    pairs = add_up(sums)
    slope = weights * (pairs - jnp.sum(weights * pairs, axis=1, keepdims=True)) * scale
    d_high, d_low = two_parts(
        spread(slope, picks) * qk_ref[...] + spread_t(slope, picks) * qkt_ref[...]
    )
    a_high, a_low = a_high_ref[...], a_low_ref[...]
    for tiles in tile_groups(first, last, half):
        e = gather_tiles(fields, tiles, per, main)
        c = gather_tiles(grads, tiles, per, main)
        value = (
            mm(d_high, e, ((1,), (0,))) + mm(d_low, e, ((1,), (0,)))
            + mm(a_high, c, ((1,), (0,))) + mm(a_low, c, ((1,), (0,)))
        )
        store_tiles(outs, value, tiles, per, first, last)


def finish_kernel(
    me_of, count, main, per, length, stages, halves, serial, waits, extras, *refs
):
    me = me_of()
    base, extra = refs[waits:waits + count], refs[waits + count:waits + count + extras]
    out_ref, held, sem = refs[waits + count + extras:]

    def send(slot, size, place):
        place = pl.multiple_of(place, LANES)
        copy = pltpu.make_async_copy(
            held.at[slot, :, pl.ds(0, size)], out_ref.at[:, pl.ds(place, size)], sem.at[slot]
        )
        copy.start()
        if serial:
            copy.wait()
        return copy

    slot = 0
    for number, stage in enumerate(stages):
        copies = []
        for s, begin, end, index, origin in stage:
            for tile in range(begin, end):
                mine = base[s][tile * per:(tile + 1) * per, :].astype(jnp.float32)
                more = extra[index][(tile - origin) * per:(tile - origin + 1) * per, :]
                held[slot, :, (tile - begin) * LANES:(tile - begin + 1) * LANES] = (
                    mine + more.astype(jnp.float32)
                )
            start = chunk_start(partner(me, s), main * LANES, length)
            copies.append(send(slot, (end - begin) * LANES, start + begin * LANES))
            slot += 1
        if halves and number == len(stages) - 1:
            packed = [
                base[s][main * per:, :].astype(jnp.float32)
                + extra[index][row:, :].astype(jnp.float32)
                for s, (index, row) in enumerate(halves)
            ]
            shape = packed[0].shape
            odd = lax.broadcasted_iota(jnp.int32, shape, 1) * 0 + me % 2 == 1
            for s in range(0, count, 2):
                even_part = jnp.where(odd, packed[s + 1], packed[s])
                odd_part = jnp.where(odd, packed[s], packed[s + 1])
                left = left_half(shape)
                held[slot, :per // 2, :LANES] = jnp.where(
                    left, even_part, swap_halves(odd_part)
                )
                held[slot, per // 2:, :LANES] = jnp.where(
                    left, swap_halves(even_part), odd_part
                )
                place = (main * count + partner(me, s) // 2) * LANES
                copies.append(send(slot, LANES, place))
                slot += 1
        if not serial:
            for copy in copies:
                copy.wait()


def swap(value, step, count):
    return lax.ppermute(value, "mem", [(i, i ^ step) for i in range(count)])


def exchange(parts):
    count = len(parts)
    return [part if s == 0 else swap(part, s, count) for s, part in enumerate(parts)]


def sum_steps(value, name, steps):
    size = lax.axis_size(name)
    for step in steps:
        value = value + lax.ppermute(value, name, [(i, i ^ step) for i in range(size)])
    return value


def doubling(size):
    steps, step = [], 1
    while step < size:
        steps.append(step)
        step *= 2
    return steps


def shards(ensemble, cotangent, w_query, w_key, w_value, w_out):
    count = lax.axis_size("mem")
    group, channels, length = ensemble.shape
    members = group * count
    per = group * channels
    rows = per * count
    main, half = tile_layout(length, count)
    chunk = main * LANES + half * LANES // 2
    scale = 1.0 / (length * lax.axis_size("space") * math.sqrt(channels))
    me_of = lambda: lax.axis_index("mem")
    bf, f32 = jnp.bfloat16, jnp.float32
    whole = pl.BlockSpec(memory_space=VMEM)
    anywhere = pl.BlockSpec(memory_space=pl.ANY)
    in_hbm = pl.BlockSpec(memory_space=pltpu.MemorySpace.HBM)
    params = pltpu.CompilerParams(vmem_limit_bytes=16 * 1024 * 1024 + 24 * rows * rows)

    def packed(tiles, with_half):
        return jax.ShapeDtypeStruct((tiles * per + with_half * per // 2, LANES), bf)

    part = packed(main, half)
    square = jax.ShapeDtypeStruct((rows, rows), f32)
    pair = jax.ShapeDtypeStruct((members, members), f32)
    fields = ensemble.reshape(per, length)
    grads = cotangent.reshape(per, length)

    def cost(flops, moved):
        return pl.CostEstimate(flops=flops, bytes_accessed=moved, transcendentals=0)

    first = min(1, count - 1)

    def split(operands, name):
        return pl.pallas_call(
            functools.partial(split_kernel, me_of, count, main, half, length),
            out_shape=[part] * count,
            in_specs=[whole] + [anywhere] * (len(operands) - 1),
            out_specs=[whole] * count,
            compiler_params=params,
            name=name,
        )(*operands)

    e_mine = split([fields], "split_fields")
    e_cells = exchange(e_mine)
    qk, qkt, ov, ovt = pl.pallas_call(
        functools.partial(tiles_kernel, rows, channels),
        out_shape=[square] * 4,
        in_specs=[whole] * 4,
        out_specs=[whole] * 4,
        compiler_params=params,
        cost_estimate=cost(10**8, 4 * 4 * rows * rows),
        name="weight_tiles",
    )(w_query, w_key, w_value, w_out)
    c_mine = split([grads, e_cells[first], qk], "split_grads")
    c_cells = exchange(c_mine)
    space_steps = doubling(lax.axis_size("space"))

    def join(value, name, step, waited):
        size = lax.axis_size(name)
        other = lax.ppermute(value, name, [(i, i ^ step) for i in range(size)])
        return pl.pallas_call(
            join_kernel,
            out_shape=pair,
            in_specs=[whole] * 2 + [anywhere] * len(waited),
            out_specs=whole,
            compiler_params=params,
            cost_estimate=cost(members * members, 12 * members * members),
            name="join_sums",
        )(value, other, *waited)

    scores = pl.pallas_call(
        functools.partial(
            score_kernel, me_of, count, main, half, per, length, group, channels, members
        ),
        out_shape=pair,
        in_specs=[whole] * (count + 1),
        out_specs=whole,
        compiler_params=params,
        cost_estimate=cost(2 * rows * rows * chunk, 2 * rows * chunk),
        name="score_sums",
    )(qk, *e_cells)
    scores = sum_steps(scores, "space", space_steps[:-1])
    scores = join(scores, "space", space_steps[-1], c_cells[first:first + 1])
    order = sorted(range(1, count), key=lambda s: (s & (s - 1) == 0, s))
    score_parts = [scores] + [swap(scores, s, count) for s in order]
    waited = score_parts[:1]
    pairs = pl.pallas_call(
        functools.partial(
            pair_kernel, me_of, count, main, half, per, length, group, channels, members
        ),
        out_shape=pair,
        in_specs=[whole] * (2 * count + 1) + [anywhere] * len(waited),
        out_specs=whole,
        compiler_params=params,
        cost_estimate=cost(2 * rows * rows * chunk, 4 * rows * chunk),
        name="pair_sums",
    )(ov, *e_cells, *c_cells, *waited)
    ahead = [pairs]
    outcome = pl.pallas_call(
        functools.partial(
            branch_kernel, me_of, count, main, half, per, group, channels, members, scale, len(ahead),
        ),
        out_shape=[pair] + [part] * count,
        in_specs=[whole] * (2 * count + 1) + [anywhere] * len(ahead),
        out_specs=[whole] * (count + 1),
        compiler_params=params,
        cost_estimate=cost(4 * rows * rows * chunk, 4 * rows * chunk),
        name="branch",
    )(ov, *score_parts, *e_cells, *ahead)
    scores, branch = outcome[0], outcome[1:]
    branch_home = exchange(branch)
    pairs = sum_steps(pairs, "space", space_steps[:-1])
    pairs = join(pairs, "space", space_steps[-1], branch_home[first:first + 1])
    pair_parts = [pairs] + [swap(pairs, s, count) for s in order]

    weights, a_high, a_low = pl.pallas_call(
        functools.partial(
            transposed_weights_kernel, me_of, channels, members, group, scale
        ),
        out_shape=[pair] + [jax.ShapeDtypeStruct((rows, rows), bf)] * 2,
        in_specs=[whole] * 2,
        out_specs=[whole] * 3,
        compiler_params=params,
        cost_estimate=cost(10**8, 8 * rows * rows),
        name="transposed_weights",
    )(scores, ovt)

    def gradient(begin, end, with_half, awaited, name):
        size = (end - begin) * LANES
        parts = pl.pallas_call(
            functools.partial(
                grad_kernel, me_of, count, main, with_half, per, group, channels, members, scale,
                begin, end, len(awaited),
            ),
            out_shape=[packed(end - begin, with_half)] * count,
            in_specs=[whole] * (3 * count + 5) + [anywhere] * len(awaited),
            out_specs=[whole] * count,
            compiler_params=params,
            cost_estimate=cost(8 * rows * rows * size, 6 * rows * size),
            name=name,
        )(weights, qk, qkt, a_high, a_low, *e_cells, *c_cells, *pair_parts, *awaited)
        return exchange(parts)

    mid = (main + 1 + half) // 2
    grad_a = gradient(0, mid, 0, branch_home[1:], "input_gradient_a")
    grad_b = gradient(mid, main, half, branch_home[1:], "input_gradient_b")
    serial = count * main - length // LANES > main - mid

    def finish(base, extra, stages, halves, before, after, name):
        slots = sum(len(stage) for stage in stages) + (count // 2 if halves else 0)
        waited = list(before) + list(after)
        return pl.pallas_call(
            functools.partial(
                finish_kernel, me_of, count, main, per, length, stages, halves, serial,
                len(waited), len(extra),
            ),
            out_shape=jax.ShapeDtypeStruct((per, length), f32),
            in_specs=[anywhere] * len(waited) + [whole] * (count + len(extra)),
            out_specs=in_hbm,
            scratch_shapes=[
                pltpu.VMEM((slots, per, mid * LANES), f32),
                pltpu.SemaphoreType.DMA((slots,)),
            ],
            input_output_aliases={0: 0} if before else {},
            compiler_params=params,
            cost_estimate=cost(per * length, 8 * per * length),
            name=name,
        )(*waited, *base, *extra)

    steps = list(range(count))
    first_part = [(s, 0, mid, s, 0) for s in steps]
    updated = finish(
        e_mine, branch_home, [first_part, [(s, mid, main, s, 0) for s in steps]],
        [(s, main * per) for s in steps] if half else [], [], [grad_a[first]], "updated",
    )
    ensemble_grad = finish(
        c_mine, grad_a + grad_b[:1], [first_part, [(0, mid, main, count, mid)]],
        [], [], [], "ensemble_grad_early",
    )
    if count > 1:
        ensemble_grad = finish(
            c_mine, grad_b, [[(s, mid, main, s, mid) for s in steps[1:]]],
            [(s, (main - mid) * per) for s in steps] if half else [],
            [ensemble_grad], [], "ensemble_grad_late",
        )
    shape = (group, channels, length)
    return (updated.reshape(shape), ensemble_grad.reshape(shape))


def solution(mesh):
    split = P("mem", None, "space")
    return jax.shard_map(
        shards,
        mesh=mesh,
        in_specs=(split, split, P(), P(), P(), P()),
        out_specs=(split, split),
        check_vma=False,
    )
```

```python
import functools
import math

import jax
import jax.numpy as jnp
from jax import lax
from jax.experimental import pallas as pl
from jax.experimental.pallas import tpu as pltpu
from jax.sharding import PartitionSpec as P

LANES = 128
HIGH = lax.Precision.HIGHEST
VMEM = pltpu.MemorySpace.VMEM


def mm(a, b, dims, precision=None):
    return lax.dot_general(
        a, b, (dims, ((), ())), precision=precision, preferred_element_type=jnp.float32
    )


def chunk_start(index, chunk, length):
    return pl.multiple_of(jnp.minimum(index * chunk, length - chunk), LANES)


def partner(me, step):
    return me ^ step


def tile_layout(length, count):
    main, left = divmod(length // LANES, count)
    if left and 2 * left == count:
        return main, 1
    return main + (left > 0), 0


def tile_groups(first, last, half, most=4):
    tiles = list(range(first, last)) + [None] * half
    return [tiles[at:at + most] for at in range(0, len(tiles), most)]


def swap_halves(value):
    return pltpu.roll(value, LANES // 2, 1)


def left_half(shape):
    return lax.broadcasted_iota(jnp.int32, shape, 1) < LANES // 2


def pack(tile, odd=None):
    half = tile.shape[0] // 2
    top, low = tile[:half], tile[half:]
    left, right = top, swap_halves(low)
    if odd is not None:
        second = lax.broadcasted_iota(jnp.int32, top.shape, 1) * 0 + odd == 1
        left, right = jnp.where(second, swap_halves(top), top), jnp.where(second, low, right)
    return jnp.where(left_half(top.shape), left, right)


def tile_of(ref, tile, per, main):
    if tile is not None:
        return ref[tile * per:(tile + 1) * per, :]
    packed = ref[main * per:, :].astype(jnp.float32)
    return jnp.concatenate([packed, swap_halves(packed)], axis=0).astype(jnp.bfloat16)


def gather_tiles(refs, group, per, main):
    return jnp.concatenate(
        [
            jnp.concatenate([tile_of(ref, tile, per, main) for tile in group], axis=1)
            for ref in refs
        ],
        axis=0,
    )


def store_tiles(outs, value, group, per, first, last):
    for at, tile in enumerate(group):
        for s, out in enumerate(outs):
            rows = value[s * per:(s + 1) * per, at * LANES:(at + 1) * LANES]
            if tile is None:
                out[(last - first) * per:, :] = pack(rows).astype(jnp.bfloat16)
            else:
                out[(tile - first) * per:(tile - first + 1) * per, :] = rows.astype(
                    jnp.bfloat16
                )


def member_of_row(me, rows, channels, members, group):
    row = lax.broadcasted_iota(jnp.int32, (rows, members), 0)
    col = lax.broadcasted_iota(jnp.int32, (rows, members), 1)
    per_group = group * channels
    owner = (row // per_group) ^ me
    member = owner * group + (row % per_group) // channels
    return (member == col).astype(jnp.float32)


def split_kernel(me_of, count, main, half, length, x_ref, *rest):
    outs = rest[-count:]
    me = me_of()
    per = x_ref.shape[0]
    for s in range(count):
        owner = partner(me, s)
        start = chunk_start(owner, main * LANES, length)
        for tile in range(main):
            place = pl.multiple_of(start + tile * LANES, LANES)
            outs[s][tile * per:(tile + 1) * per, :] = x_ref[:, pl.ds(place, LANES)]
        if half:
            place = pl.multiple_of((main * count + owner // 2) * LANES, LANES)
            shared = x_ref[:, pl.ds(place, LANES)].astype(jnp.float32)
            outs[s][main * per:, :] = pack(shared, owner % 2).astype(jnp.bfloat16)


def tiled(small, rows, channels):
    tall = jnp.concatenate([small] * (rows // channels), axis=0)
    col = lax.broadcasted_iota(jnp.int32, (channels, rows), 1)
    row = lax.broadcasted_iota(jnp.int32, (channels, rows), 0)
    spread = (col % channels == row).astype(jnp.float32)
    return mm(tall, spread, ((1,), (0,)), HIGH)


def tiles_kernel(rows, channels, wq_ref, wk_ref, wv_ref, wo_ref, qk_ref, qkt_ref, ov_ref, ovt_ref):
    wq, wk = wq_ref[...].astype(jnp.float32), wk_ref[...].astype(jnp.float32)
    wv, wo = wv_ref[...].astype(jnp.float32), wo_ref[...].astype(jnp.float32)
    wqt, wkt, wvt, wot = wq.T, wk.T, wv.T, wo.T
    qk_ref[...] = tiled(mm(wqt, wk, ((1,), (0,)), HIGH), rows, channels)
    qkt_ref[...] = tiled(mm(wkt, wq, ((1,), (0,)), HIGH), rows, channels)
    ov_ref[...] = tiled(mm(wo, wv, ((1,), (0,)), HIGH), rows, channels)
    ovt_ref[...] = tiled(mm(wvt, wot, ((1,), (0,)), HIGH), rows, channels)


def three_parts(value):
    parts = []
    for _ in range(3):
        parts.append(value.astype(jnp.bfloat16))
        value = value - parts[-1].astype(jnp.float32)
    return parts


def fold(me, weighted, channels, members, group):
    rows = weighted.shape[0]
    half = jnp.sum(weighted.reshape(members, channels, rows), axis=1)
    picks = member_of_row(me, rows, channels, members, group).astype(jnp.bfloat16)
    half = sum(mm(part, picks, ((1,), (0,))) for part in three_parts(half))
    local = lax.broadcasted_iota(jnp.int32, (members, members), 1)
    member = lax.broadcasted_iota(jnp.int32, (members, members), 0)
    order = (((local // group) ^ me) * group + local % group == member).astype(jnp.bfloat16)
    return sum(mm(order, part, ((1,), (0,))) for part in three_parts(half))


def masked_gram(me, count, main, half, per, length, left, right):
    rows = count * per
    chunk = main * LANES
    skip = me * chunk - chunk_start(me, chunk, length)
    most = max(0, count * chunk - length)
    total = jnp.zeros((rows, rows), jnp.float32)
    at = 0
    for group in tile_groups(0, main, half):
        b = gather_tiles(right, group, per, main)
        a = b if left is right else gather_tiles(left, group, per, main)
        if at < most or None in group:
            lane = lax.broadcasted_iota(jnp.int32, a.shape, 1) + at
            valid = (lane >= skip) & (lane < chunk + LANES // 2)
            a = jnp.where(valid, a.astype(jnp.float32), 0.0).astype(jnp.bfloat16)
        total = total + mm(a, b, ((1,), (1,)))
        at += len(group) * LANES
    return total


def score_kernel(me_of, count, main, half, per, length, group, channels, members, tile_ref, *refs):
    me = me_of()
    fields, out_ref = refs[:count], refs[-1]
    total = masked_gram(me, count, main, half, per, length, fields, fields)
    out_ref[...] = fold(me, total * tile_ref[...], channels, members, group)


def pair_kernel(me_of, count, main, half, per, length, group, channels, members, tile_ref, *refs):
    me = me_of()
    fields, grads, out_ref = refs[:count], refs[count:2 * count], refs[-1]
    total = masked_gram(me, count, main, half, per, length, grads, fields)
    out_ref[...] = fold(me, total * tile_ref[...], channels, members, group)


def add_up(refs):
    return functools.reduce(jnp.add, [r[...] for r in refs])


def join_kernel(a_ref, b_ref, *refs):
    refs[-1][...] = a_ref[...] + b_ref[...]


def softmax(scores):
    peak = jnp.max(scores, axis=1, keepdims=True)
    exponent = jnp.exp(scores - peak)
    return exponent / jnp.sum(exponent, axis=1, keepdims=True)


def spread(small, picks):
    tall = mm(picks, small.astype(jnp.bfloat16), ((1,), (0,))).astype(jnp.bfloat16)
    return mm(tall, picks, ((1,), (1,)))


def spread_t(small, picks):
    tall = mm(picks, small.astype(jnp.bfloat16), ((1,), (1,))).astype(jnp.bfloat16)
    return mm(tall, picks, ((1,), (1,)))


def two_parts(value):
    high = value.astype(jnp.bfloat16)
    return high, (value - high.astype(jnp.float32)).astype(jnp.bfloat16)


def branch_kernel(
    me_of, count, main, half, per, group, channels, members, scale, waits, ov_ref, *refs
):
    me = me_of()
    sums, fields = refs[:count], refs[count:2 * count]
    total_ref, outs = refs[2 * count + waits], refs[2 * count + waits + 1:]
    rows = count * per
    total = add_up(sums)
    total_ref[...] = total
    picks = member_of_row(me, rows, channels, members, group).astype(jnp.bfloat16)
    weights = softmax(total * scale)
    high, low = two_parts(spread(weights, picks) * ov_ref[...])
    for tiles in tile_groups(0, main, half):
        e = gather_tiles(fields, tiles, per, main)
        value = mm(high, e, ((1,), (0,))) + mm(low, e, ((1,), (0,)))
        store_tiles(outs, value, tiles, per, 0, main)


def early_gradient_kernel(
    me_of, count, main, per, last, channels, members, group, scale, s_ref, ovt_ref, *refs
):
    grads, (w_ref, high_ref, low_ref, value_ref) = refs[:count], refs[count:]
    rows = ovt_ref.shape[0]
    picks = member_of_row(me_of(), rows, channels, members, group).astype(jnp.bfloat16)
    weights = softmax(s_ref[...] * scale)
    w_ref[...] = weights
    high, low = two_parts(spread_t(weights, picks) * ovt_ref[...])
    high_ref[...], low_ref[...] = high, low
    at = 0
    for tiles in tile_groups(0, last, 0):
        c = gather_tiles(grads, tiles, per, main)
        value_ref[:, at:at + len(tiles) * LANES] = mm(high, c, ((1,), (0,))) + mm(
            low, c, ((1,), (0,))
        )
        at += len(tiles) * LANES


def grad_kernel(
    me_of, count, main, half, per, group, channels, members, scale, first, last, waits, early,
    w_ref, qk_ref, qkt_ref, *refs,
):
    me = me_of()
    known, refs = refs[:1 if early else 2], refs[1 if early else 2:]
    fields, grads, sums = refs[:count], refs[count:2 * count], refs[2 * count:3 * count]
    outs = refs[3 * count + waits:]
    rows = count * per
    picks = member_of_row(me, rows, channels, members, group).astype(jnp.bfloat16)
    weights = w_ref[...]
    pairs = add_up(sums)
    slope = weights * (pairs - jnp.sum(weights * pairs, axis=1, keepdims=True)) * scale
    d_high, d_low = two_parts(
        spread(slope, picks) * qk_ref[...] + spread_t(slope, picks) * qkt_ref[...]
    )
    at = 0
    for tiles in tile_groups(first, last, half):
        e = gather_tiles(fields, tiles, per, main)
        value = mm(d_high, e, ((1,), (0,))) + mm(d_low, e, ((1,), (0,)))
        if early:
            value = value + known[0][:, at:at + len(tiles) * LANES]
        else:
            c = gather_tiles(grads, tiles, per, main)
            for weight in known:
                value = value + mm(weight[...], c, ((1,), (0,)))
        store_tiles(outs, value, tiles, per, first, last)
        at += len(tiles) * LANES


def finish_kernel(
    me_of, count, main, per, length, stages, halves, serial, waits, extras, *refs
):
    me = me_of()
    base, extra = refs[waits:waits + count], refs[waits + count:waits + count + extras]
    out_ref, held, sem = refs[waits + count + extras:]

    def send(slot, size, place):
        place = pl.multiple_of(place, LANES)
        copy = pltpu.make_async_copy(
            held.at[slot, :, pl.ds(0, size)], out_ref.at[:, pl.ds(place, size)], sem.at[slot]
        )
        copy.start()
        if serial:
            copy.wait()
        return copy

    slot = 0
    for number, stage in enumerate(stages):
        copies = []
        for s, begin, end, index, origin in stage:
            for tile in range(begin, end):
                mine = base[s][tile * per:(tile + 1) * per, :].astype(jnp.float32)
                more = extra[index][(tile - origin) * per:(tile - origin + 1) * per, :]
                held[slot, :, (tile - begin) * LANES:(tile - begin + 1) * LANES] = (
                    mine + more.astype(jnp.float32)
                )
            start = chunk_start(partner(me, s), main * LANES, length)
            copies.append(send(slot, (end - begin) * LANES, start + begin * LANES))
            slot += 1
        if halves and number == len(stages) - 1:
            packed = [
                base[s][main * per:, :].astype(jnp.float32)
                + extra[index][row:, :].astype(jnp.float32)
                for s, (index, row) in enumerate(halves)
            ]
            shape = packed[0].shape
            odd = lax.broadcasted_iota(jnp.int32, shape, 1) * 0 + me % 2 == 1
            for s in range(0, count, 2):
                even_part = jnp.where(odd, packed[s + 1], packed[s])
                odd_part = jnp.where(odd, packed[s], packed[s + 1])
                left = left_half(shape)
                held[slot, :per // 2, :LANES] = jnp.where(
                    left, even_part, swap_halves(odd_part)
                )
                held[slot, per // 2:, :LANES] = jnp.where(
                    left, swap_halves(even_part), odd_part
                )
                place = (main * count + partner(me, s) // 2) * LANES
                copies.append(send(slot, LANES, place))
                slot += 1
        if not serial:
            for copy in copies:
                copy.wait()


def swap(value, step, count):
    return lax.ppermute(value, "mem", [(i, i ^ step) for i in range(count)])


def exchange(parts):
    count = len(parts)
    return [part if s == 0 else swap(part, s, count) for s, part in enumerate(parts)]


def sum_steps(value, name, steps):
    size = lax.axis_size(name)
    for step in steps:
        value = value + lax.ppermute(value, name, [(i, i ^ step) for i in range(size)])
    return value


def doubling(size):
    steps, step = [], 1
    while step < size:
        steps.append(step)
        step *= 2
    return steps


def shards(ensemble, cotangent, w_query, w_key, w_value, w_out):
    count = lax.axis_size("mem")
    group, channels, length = ensemble.shape
    members = group * count
    per = group * channels
    rows = per * count
    main, half = tile_layout(length, count)
    chunk = main * LANES + half * LANES // 2
    scale = 1.0 / (length * lax.axis_size("space") * math.sqrt(channels))
    me_of = lambda: lax.axis_index("mem")
    bf, f32 = jnp.bfloat16, jnp.float32
    whole = pl.BlockSpec(memory_space=VMEM)
    anywhere = pl.BlockSpec(memory_space=pl.ANY)
    in_hbm = pl.BlockSpec(memory_space=pltpu.MemorySpace.HBM)
    params = pltpu.CompilerParams(vmem_limit_bytes=16 * 1024 * 1024 + 24 * rows * rows)

    def packed(tiles, with_half):
        return jax.ShapeDtypeStruct((tiles * per + with_half * per // 2, LANES), bf)

    part = packed(main, half)
    square = jax.ShapeDtypeStruct((rows, rows), f32)
    pair = jax.ShapeDtypeStruct((members, members), f32)
    fields = ensemble.reshape(per, length)
    grads = cotangent.reshape(per, length)

    def cost(flops, moved):
        return pl.CostEstimate(flops=flops, bytes_accessed=moved, transcendentals=0)

    first = min(1, count - 1)

    def split(operands, name):
        return pl.pallas_call(
            functools.partial(split_kernel, me_of, count, main, half, length),
            out_shape=[part] * count,
            in_specs=[whole] + [anywhere] * (len(operands) - 1),
            out_specs=[whole] * count,
            compiler_params=params,
            name=name,
        )(*operands)

    e_mine = split([fields], "split_fields")
    e_cells = exchange(e_mine)
    qk, qkt, ov, ovt = pl.pallas_call(
        functools.partial(tiles_kernel, rows, channels),
        out_shape=[square] * 4,
        in_specs=[whole] * 4,
        out_specs=[whole] * 4,
        compiler_params=params,
        cost_estimate=cost(10**8, 4 * 4 * rows * rows),
        name="weight_tiles",
    )(w_query, w_key, w_value, w_out)
    c_mine = split([grads, e_cells[first], qk], "split_grads")
    c_cells = exchange(c_mine)
    space_steps = doubling(lax.axis_size("space"))

    def join(value, name, step, waited):
        size = lax.axis_size(name)
        other = lax.ppermute(value, name, [(i, i ^ step) for i in range(size)])
        return pl.pallas_call(
            join_kernel,
            out_shape=pair,
            in_specs=[whole] * 2 + [anywhere] * len(waited),
            out_specs=whole,
            compiler_params=params,
            cost_estimate=cost(members * members, 12 * members * members),
            name="join_sums",
        )(value, other, *waited)

    scores = pl.pallas_call(
        functools.partial(
            score_kernel, me_of, count, main, half, per, length, group, channels, members
        ),
        out_shape=pair,
        in_specs=[whole] * (count + 1),
        out_specs=whole,
        compiler_params=params,
        cost_estimate=cost(2 * rows * rows * chunk, 2 * rows * chunk),
        name="score_sums",
    )(qk, *e_cells)
    scores = sum_steps(scores, "space", space_steps[:-1])
    scores = join(scores, "space", space_steps[-1], c_cells[first:first + 1])
    order = sorted(range(1, count), key=lambda s: (s & (s - 1) == 0, s))
    score_parts = [scores] + [swap(scores, s, count) for s in order]
    waited = score_parts[:1]
    pairs = pl.pallas_call(
        functools.partial(
            pair_kernel, me_of, count, main, half, per, length, group, channels, members
        ),
        out_shape=pair,
        in_specs=[whole] * (2 * count + 1) + [anywhere] * len(waited),
        out_specs=whole,
        compiler_params=params,
        cost_estimate=cost(2 * rows * rows * chunk, 4 * rows * chunk),
        name="pair_sums",
    )(ov, *e_cells, *c_cells, *waited)
    ahead = [pairs]
    outcome = pl.pallas_call(
        functools.partial(
            branch_kernel, me_of, count, main, half, per, group, channels, members, scale, len(ahead),
        ),
        out_shape=[pair] + [part] * count,
        in_specs=[whole] * (2 * count + 1) + [anywhere] * len(ahead),
        out_specs=[whole] * (count + 1),
        compiler_params=params,
        cost_estimate=cost(4 * rows * rows * chunk, 4 * rows * chunk),
        name="branch",
    )(ov, *score_parts, *e_cells, *ahead)
    scores, branch = outcome[0], outcome[1:]
    branch_home = exchange(branch)
    pairs = sum_steps(pairs, "space", space_steps[:-1])
    pairs = join(pairs, "space", space_steps[-1], branch_home[first:first + 1])
    pair_parts = [pairs] + [swap(pairs, s, count) for s in order]

    mid = (main + 1 + half) // 2
    weights, a_high, a_low, early = pl.pallas_call(
        functools.partial(
            early_gradient_kernel, me_of, count, main, per, mid, channels, members, group,
            scale,
        ),
        out_shape=[pair]
        + [jax.ShapeDtypeStruct((rows, rows), bf)] * 2
        + [jax.ShapeDtypeStruct((rows, mid * LANES), f32)],
        in_specs=[whole] * (count + 2),
        out_specs=[whole] * 4,
        compiler_params=params,
        cost_estimate=cost(10**8, 8 * rows * rows),
        name="early_gradient",
    )(scores, ovt, *c_cells)

    def gradient(begin, end, with_half, known, awaited, name):
        size = (end - begin) * LANES
        parts = pl.pallas_call(
            functools.partial(
                grad_kernel, me_of, count, main, with_half, per, group, channels, members, scale,
                begin, end, len(awaited), len(known) == 1,
            ),
            out_shape=[packed(end - begin, with_half)] * count,
            in_specs=[whole] * (3 * count + 3 + len(known)) + [anywhere] * len(awaited),
            out_specs=[whole] * count,
            compiler_params=params,
            cost_estimate=cost(8 * rows * rows * size, 6 * rows * size),
            name=name,
        )(weights, qk, qkt, *known, *e_cells, *c_cells, *pair_parts, *awaited)
        return exchange(parts)

    grad_a = gradient(0, mid, 0, [early], branch_home[1:], "input_gradient_a")
    grad_b = gradient(mid, main, half, [a_high, a_low], branch_home[1:], "input_gradient_b")
    serial = count * main - length // LANES > main - mid

    def finish(base, extra, stages, halves, before, after, name):
        slots = sum(len(stage) for stage in stages) + (count // 2 if halves else 0)
        waited = list(before) + list(after)
        return pl.pallas_call(
            functools.partial(
                finish_kernel, me_of, count, main, per, length, stages, halves, serial,
                len(waited), len(extra),
            ),
            out_shape=jax.ShapeDtypeStruct((per, length), f32),
            in_specs=[anywhere] * len(waited) + [whole] * (count + len(extra)),
            out_specs=in_hbm,
            scratch_shapes=[
                pltpu.VMEM((slots, per, mid * LANES), f32),
                pltpu.SemaphoreType.DMA((slots,)),
            ],
            input_output_aliases={0: 0} if before else {},
            compiler_params=params,
            cost_estimate=cost(per * length, 8 * per * length),
            name=name,
        )(*waited, *base, *extra)

    steps = list(range(count))
    first_part = [(s, 0, mid, s, 0) for s in steps]
    updated = finish(
        e_mine, branch_home, [first_part, [(s, mid, main, s, 0) for s in steps]],
        [(s, main * per) for s in steps] if half else [], [], [grad_a[first]], "updated",
    )
    ensemble_grad = finish(
        c_mine, grad_a + grad_b[:1], [first_part, [(0, mid, main, count, mid)]],
        [], [], [], "ensemble_grad_early",
    )
    if count > 1:
        ensemble_grad = finish(
            c_mine, grad_b, [[(s, mid, main, s, mid) for s in steps[1:]]],
            [(s, (main - mid) * per) for s in steps] if half else [],
            [ensemble_grad], [], "ensemble_grad_late",
        )
    shape = (group, channels, length)
    return (updated.reshape(shape), ensemble_grad.reshape(shape))


def solution(mesh):
    split = P("mem", None, "space")
    return jax.shard_map(
        shards,
        mesh=mesh,
        in_specs=(split, split, P(), P(), P(), P()),
        out_specs=(split, split),
        check_vma=False,
    )
```

```python
import functools
import math

import jax
import jax.numpy as jnp
from jax import lax
from jax.experimental import pallas as pl
from jax.experimental.pallas import tpu as pltpu
from jax.sharding import PartitionSpec as P

LANES = 128
HIGH = lax.Precision.HIGHEST
VMEM = pltpu.MemorySpace.VMEM


def mm(a, b, dims, precision=None):
    return lax.dot_general(
        a, b, (dims, ((), ())), precision=precision, preferred_element_type=jnp.float32
    )


def chunk_start(index, chunk, length):
    return pl.multiple_of(jnp.minimum(index * chunk, length - chunk), LANES)


def partner(me, step):
    return me ^ step


def tile_layout(length, count):
    main, left = divmod(length // LANES, count)
    if left and 2 * left == count:
        return main, 1
    return main + (left > 0), 0


def tile_groups(first, last, half, most=4):
    tiles = list(range(first, last)) + [None] * half
    return [tiles[at:at + most] for at in range(0, len(tiles), most)]


def swap_halves(value):
    return pltpu.roll(value, LANES // 2, 1)


def left_half(shape):
    return lax.broadcasted_iota(jnp.int32, shape, 1) < LANES // 2


def pack(tile, odd=None):
    half = tile.shape[0] // 2
    top, low = tile[:half], tile[half:]
    left, right = top, swap_halves(low)
    if odd is not None:
        second = lax.broadcasted_iota(jnp.int32, top.shape, 1) * 0 + odd == 1
        left, right = jnp.where(second, swap_halves(top), top), jnp.where(second, low, right)
    return jnp.where(left_half(top.shape), left, right)


def tile_of(ref, tile, per, main):
    if tile is not None:
        return ref[tile * per:(tile + 1) * per, :]
    packed = ref[main * per:, :].astype(jnp.float32)
    return jnp.concatenate([packed, swap_halves(packed)], axis=0).astype(jnp.bfloat16)


def gather_tiles(refs, group, per, main):
    return jnp.concatenate(
        [
            jnp.concatenate([tile_of(ref, tile, per, main) for tile in group], axis=1)
            for ref in refs
        ],
        axis=0,
    )


def store_tiles(outs, value, group, per, first, last):
    for at, tile in enumerate(group):
        for s, out in enumerate(outs):
            rows = value[s * per:(s + 1) * per, at * LANES:(at + 1) * LANES]
            if tile is None:
                out[(last - first) * per:, :] = pack(rows).astype(jnp.bfloat16)
            else:
                out[(tile - first) * per:(tile - first + 1) * per, :] = rows.astype(
                    jnp.bfloat16
                )


def member_of_row(me, rows, channels, members, group):
    row = lax.broadcasted_iota(jnp.int32, (rows, members), 0)
    col = lax.broadcasted_iota(jnp.int32, (rows, members), 1)
    per_group = group * channels
    owner = (row // per_group) ^ me
    member = owner * group + (row % per_group) // channels
    return (member == col).astype(jnp.float32)


def split_kernel(me_of, steps, count, main, half, length, x_ref, *rest):
    outs = rest[-len(steps):]
    me = me_of()
    per = x_ref.shape[0]
    for out, s in zip(outs, steps):
        owner = partner(me, s)
        start = chunk_start(owner, main * LANES, length)
        for tile in range(main):
            place = pl.multiple_of(start + tile * LANES, LANES)
            out[tile * per:(tile + 1) * per, :] = x_ref[:, pl.ds(place, LANES)]
        if half:
            place = pl.multiple_of((main * count + owner // 2) * LANES, LANES)
            shared = x_ref[:, pl.ds(place, LANES)].astype(jnp.float32)
            out[main * per:, :] = pack(shared, owner % 2).astype(jnp.bfloat16)


def direct_split_kernel(me_of, steps, count, main, half, length, x_ref, *rest):
    outs, (held, shared, sem) = rest[:len(steps)], rest[len(steps):]
    me = me_of()
    per = x_ref.shape[0]
    copies = []
    for at, s in enumerate(steps):
        owner = partner(me, s)
        start = chunk_start(owner, main * LANES, length)
        copies.append(pltpu.make_async_copy(
            x_ref.at[:, pl.ds(start, main * LANES)], held.at[at], sem.at[2 * at]
        ))
        if half:
            place = pl.multiple_of((main * count + owner // 2) * LANES, LANES)
            copies.append(pltpu.make_async_copy(
                x_ref.at[:, pl.ds(place, LANES)], shared.at[at], sem.at[2 * at + 1]
            ))
    for copy in copies:
        copy.start()
    for copy in copies:
        copy.wait()
    for at, s in enumerate(steps):
        for tile in range(main):
            outs[at][tile * per:(tile + 1) * per, :] = held[
                at, :, tile * LANES:(tile + 1) * LANES
            ]
        if half:
            tile = shared[at].astype(jnp.float32)
            outs[at][main * per:, :] = pack(tile, partner(me, s) % 2).astype(jnp.bfloat16)


def tiled(small, rows, channels):
    tall = jnp.concatenate([small] * (rows // channels), axis=0)
    col = lax.broadcasted_iota(jnp.int32, (channels, rows), 1)
    row = lax.broadcasted_iota(jnp.int32, (channels, rows), 0)
    spread = (col % channels == row).astype(jnp.float32)
    return mm(tall, spread, ((1,), (0,)), HIGH)


def tiles_kernel(rows, channels, wq_ref, wk_ref, wv_ref, wo_ref, qk_ref, qkt_ref, ov_ref, ovt_ref):
    wq, wk = wq_ref[...].astype(jnp.float32), wk_ref[...].astype(jnp.float32)
    wv, wo = wv_ref[...].astype(jnp.float32), wo_ref[...].astype(jnp.float32)
    wqt, wkt, wvt, wot = wq.T, wk.T, wv.T, wo.T
    qk_ref[...] = tiled(mm(wqt, wk, ((1,), (0,)), HIGH), rows, channels)
    qkt_ref[...] = tiled(mm(wkt, wq, ((1,), (0,)), HIGH), rows, channels)
    ov_ref[...] = tiled(mm(wo, wv, ((1,), (0,)), HIGH), rows, channels)
    ovt_ref[...] = tiled(mm(wvt, wot, ((1,), (0,)), HIGH), rows, channels)


def three_parts(value):
    parts = []
    for _ in range(3):
        parts.append(value.astype(jnp.bfloat16))
        value = value - parts[-1].astype(jnp.float32)
    return parts


def fold(me, weighted, channels, members, group):
    rows = weighted.shape[0]
    half = jnp.sum(weighted.reshape(members, channels, rows), axis=1)
    picks = member_of_row(me, rows, channels, members, group).astype(jnp.bfloat16)
    half = sum(mm(part, picks, ((1,), (0,))) for part in three_parts(half))
    local = lax.broadcasted_iota(jnp.int32, (members, members), 1)
    member = lax.broadcasted_iota(jnp.int32, (members, members), 0)
    order = (((local // group) ^ me) * group + local % group == member).astype(jnp.bfloat16)
    return sum(mm(order, part, ((1,), (0,))) for part in three_parts(half))


def masked_gram(me, count, main, half, per, length, left, right):
    rows = count * per
    chunk = main * LANES
    skip = me * chunk - chunk_start(me, chunk, length)
    most = max(0, count * chunk - length)
    total = jnp.zeros((rows, rows), jnp.float32)
    at = 0
    for group in tile_groups(0, main, half):
        b = gather_tiles(right, group, per, main)
        a = b if left is right else gather_tiles(left, group, per, main)
        if at < most or None in group:
            lane = lax.broadcasted_iota(jnp.int32, a.shape, 1) + at
            valid = (lane >= skip) & (lane < chunk + LANES // 2)
            a = jnp.where(valid, a.astype(jnp.float32), 0.0).astype(jnp.bfloat16)
        total = total + mm(a, b, ((1,), (1,)))
        at += len(group) * LANES
    return total


def score_kernel(me_of, count, main, half, per, length, group, channels, members, tile_ref, *refs):
    me = me_of()
    fields, out_ref = refs[:count], refs[-1]
    total = masked_gram(me, count, main, half, per, length, fields, fields)
    out_ref[...] = fold(me, total * tile_ref[...], channels, members, group)


def pair_kernel(me_of, count, main, half, per, length, group, channels, members, tile_ref, *refs):
    me = me_of()
    fields, grads, out_ref = refs[:count], refs[count:2 * count], refs[-1]
    total = masked_gram(me, count, main, half, per, length, grads, fields)
    out_ref[...] = fold(me, total * tile_ref[...], channels, members, group)


def add_up(refs):
    return functools.reduce(jnp.add, [r[...] for r in refs])


def join_kernel(a_ref, b_ref, *refs):
    refs[-1][...] = a_ref[...] + b_ref[...]


def softmax(scores):
    peak = jnp.max(scores, axis=1, keepdims=True)
    exponent = jnp.exp(scores - peak)
    return exponent / jnp.sum(exponent, axis=1, keepdims=True)


def spread(small, picks):
    tall = mm(picks, small.astype(jnp.bfloat16), ((1,), (0,))).astype(jnp.bfloat16)
    return mm(tall, picks, ((1,), (1,)))


def spread_t(small, picks):
    tall = mm(picks, small.astype(jnp.bfloat16), ((1,), (1,))).astype(jnp.bfloat16)
    return mm(tall, picks, ((1,), (1,)))


def two_parts(value):
    high = value.astype(jnp.bfloat16)
    return high, (value - high.astype(jnp.float32)).astype(jnp.bfloat16)


def branch_kernel(
    me_of, count, main, half, per, group, channels, members, scale, waits, ov_ref, *refs
):
    me = me_of()
    sums, fields = refs[:count], refs[count:2 * count]
    total_ref, outs = refs[2 * count + waits], refs[2 * count + waits + 1:]
    rows = count * per
    total = add_up(sums)
    total_ref[...] = total
    picks = member_of_row(me, rows, channels, members, group).astype(jnp.bfloat16)
    weights = softmax(total * scale)
    high, low = two_parts(spread(weights, picks) * ov_ref[...])
    for tiles in tile_groups(0, main, half):
        e = gather_tiles(fields, tiles, per, main)
        value = mm(high, e, ((1,), (0,))) + mm(low, e, ((1,), (0,)))
        store_tiles(outs, value, tiles, per, 0, main)


def early_gradient_kernel(
    me_of, count, main, per, last, channels, members, group, scale, s_ref, ovt_ref, *refs
):
    grads, (w_ref, high_ref, low_ref, value_ref) = refs[:count], refs[count:]
    rows = ovt_ref.shape[0]
    picks = member_of_row(me_of(), rows, channels, members, group).astype(jnp.bfloat16)
    weights = softmax(s_ref[...] * scale)
    w_ref[...] = weights
    high, low = two_parts(spread_t(weights, picks) * ovt_ref[...])
    high_ref[...], low_ref[...] = high, low
    at = 0
    for tiles in tile_groups(0, last, 0):
        c = gather_tiles(grads, tiles, per, main)
        value_ref[:, at:at + len(tiles) * LANES] = mm(high, c, ((1,), (0,))) + mm(
            low, c, ((1,), (0,))
        )
        at += len(tiles) * LANES


def grad_kernel(
    me_of, count, main, half, per, group, channels, members, scale, first, last, waits, early,
    w_ref, qk_ref, qkt_ref, *refs,
):
    me = me_of()
    known, refs = refs[:1 if early else 2], refs[1 if early else 2:]
    fields, grads, sums = refs[:count], refs[count:2 * count], refs[2 * count:3 * count]
    outs = refs[3 * count + waits:]
    rows = count * per
    picks = member_of_row(me, rows, channels, members, group).astype(jnp.bfloat16)
    weights = w_ref[...]
    pairs = add_up(sums)
    slope = weights * (pairs - jnp.sum(weights * pairs, axis=1, keepdims=True)) * scale
    d_high, d_low = two_parts(
        spread(slope, picks) * qk_ref[...] + spread_t(slope, picks) * qkt_ref[...]
    )
    at = 0
    for tiles in tile_groups(first, last, half):
        e = gather_tiles(fields, tiles, per, main)
        value = mm(d_high, e, ((1,), (0,))) + mm(d_low, e, ((1,), (0,)))
        if early:
            value = value + known[0][:, at:at + len(tiles) * LANES]
        else:
            c = gather_tiles(grads, tiles, per, main)
            for weight in known:
                value = value + mm(weight[...], c, ((1,), (0,)))
        store_tiles(outs, value, tiles, per, first, last)
        at += len(tiles) * LANES


def finish_kernel(
    me_of, count, main, per, length, stages, halves, serial, waits, extras, *refs
):
    me = me_of()
    base, extra = refs[waits:waits + count], refs[waits + count:waits + count + extras]
    out_ref, held, sem = refs[waits + count + extras:]

    def send(slot, size, place):
        place = pl.multiple_of(place, LANES)
        copy = pltpu.make_async_copy(
            held.at[slot, :, pl.ds(0, size)], out_ref.at[:, pl.ds(place, size)], sem.at[slot]
        )
        copy.start()
        if serial:
            copy.wait()
        return copy

    slot = 0
    for number, stage in enumerate(stages):
        copies = []
        for s, begin, end, index, origin in stage:
            for tile in range(begin, end):
                mine = base[s][tile * per:(tile + 1) * per, :].astype(jnp.float32)
                more = extra[index][(tile - origin) * per:(tile - origin + 1) * per, :]
                held[slot, :, (tile - begin) * LANES:(tile - begin + 1) * LANES] = (
                    mine + more.astype(jnp.float32)
                )
            start = chunk_start(partner(me, s), main * LANES, length)
            copies.append(send(slot, (end - begin) * LANES, start + begin * LANES))
            slot += 1
        if halves and number == len(stages) - 1:
            packed = [
                base[s][main * per:, :].astype(jnp.float32)
                + extra[index][row:, :].astype(jnp.float32)
                for s, (index, row) in enumerate(halves)
            ]
            shape = packed[0].shape
            odd = lax.broadcasted_iota(jnp.int32, shape, 1) * 0 + me % 2 == 1
            for s in range(0, count, 2):
                even_part = jnp.where(odd, packed[s + 1], packed[s])
                odd_part = jnp.where(odd, packed[s], packed[s + 1])
                left = left_half(shape)
                held[slot, :per // 2, :LANES] = jnp.where(
                    left, even_part, swap_halves(odd_part)
                )
                held[slot, per // 2:, :LANES] = jnp.where(
                    left, swap_halves(even_part), odd_part
                )
                place = (main * count + partner(me, s) // 2) * LANES
                copies.append(send(slot, LANES, place))
                slot += 1
        if not serial:
            for copy in copies:
                copy.wait()


def swap(value, step, count):
    return lax.ppermute(value, "mem", [(i, i ^ step) for i in range(count)])


def exchange(parts):
    count = len(parts)
    return [part if s == 0 else swap(part, s, count) for s, part in enumerate(parts)]


def sum_steps(value, name, steps):
    size = lax.axis_size(name)
    for step in steps:
        value = value + lax.ppermute(value, name, [(i, i ^ step) for i in range(size)])
    return value


def doubling(size):
    steps, step = [], 1
    while step < size:
        steps.append(step)
        step *= 2
    return steps


def shards(ensemble, cotangent, w_query, w_key, w_value, w_out):
    count = lax.axis_size("mem")
    group, channels, length = ensemble.shape
    members = group * count
    per = group * channels
    rows = per * count
    main, half = tile_layout(length, count)
    chunk = main * LANES + half * LANES // 2
    scale = 1.0 / (length * lax.axis_size("space") * math.sqrt(channels))
    me_of = lambda: lax.axis_index("mem")
    bf, f32 = jnp.bfloat16, jnp.float32
    whole = pl.BlockSpec(memory_space=VMEM)
    anywhere = pl.BlockSpec(memory_space=pl.ANY)
    in_hbm = pl.BlockSpec(memory_space=pltpu.MemorySpace.HBM)
    params = pltpu.CompilerParams(vmem_limit_bytes=16 * 1024 * 1024 + 24 * rows * rows)

    def packed(tiles, with_half):
        return jax.ShapeDtypeStruct((tiles * per + with_half * per // 2, LANES), bf)

    part = packed(main, half)
    square = jax.ShapeDtypeStruct((rows, rows), f32)
    pair = jax.ShapeDtypeStruct((members, members), f32)
    fields = ensemble.reshape(per, length)
    grads = cotangent.reshape(per, length)

    def cost(flops, moved):
        return pl.CostEstimate(flops=flops, bytes_accessed=moved, transcendentals=0)

    first = min(1, count - 1)

    def split(operands, steps, name):
        return pl.pallas_call(
            functools.partial(split_kernel, me_of, steps, count, main, half, length),
            out_shape=[part] * len(steps),
            in_specs=[whole] + [anywhere] * (len(operands) - 1),
            out_specs=[whole] * len(steps),
            compiler_params=params,
            name=name,
        )(*operands)

    steps = list(range(count))
    ends = sorted({0, count - 1})
    middle = steps[1:-1]
    near = []
    if middle:
        near = list(pl.pallas_call(
            functools.partial(
                direct_split_kernel, me_of, middle, count, main, half, length
            ),
            out_shape=[part] * len(middle),
            in_specs=[in_hbm],
            out_specs=[whole] * len(middle),
            scratch_shapes=[
                pltpu.VMEM((len(middle), per, main * LANES), bf),
                pltpu.VMEM((len(middle), per, LANES), bf),
                pltpu.SemaphoreType.DMA((2 * len(middle),)),
            ],
            compiler_params=params,
            name="split_fields_near",
        )(pltpu.with_memory_space_constraint(fields, pltpu.HBM)))
    far = list(split([fields] + near[:1], ends, "split_fields_far"))
    e_mine = far[:1] + near + far[1:]
    e_cells = exchange(e_mine)
    qk, qkt, ov, ovt = pl.pallas_call(
        functools.partial(tiles_kernel, rows, channels),
        out_shape=[square] * 4,
        in_specs=[whole] * 4,
        out_specs=[whole] * 4,
        compiler_params=params,
        cost_estimate=cost(10**8, 4 * 4 * rows * rows),
        name="weight_tiles",
    )(w_query, w_key, w_value, w_out)
    c_mine = split([grads, e_cells[first], qk], steps, "split_grads")
    c_cells = exchange(c_mine)
    space_steps = doubling(lax.axis_size("space"))

    def join(value, name, step, waited):
        size = lax.axis_size(name)
        other = lax.ppermute(value, name, [(i, i ^ step) for i in range(size)])
        return pl.pallas_call(
            join_kernel,
            out_shape=pair,
            in_specs=[whole] * 2 + [anywhere] * len(waited),
            out_specs=whole,
            compiler_params=params,
            cost_estimate=cost(members * members, 12 * members * members),
            name="join_sums",
        )(value, other, *waited)

    scores = pl.pallas_call(
        functools.partial(
            score_kernel, me_of, count, main, half, per, length, group, channels, members
        ),
        out_shape=pair,
        in_specs=[whole] * (count + 1),
        out_specs=whole,
        compiler_params=params,
        cost_estimate=cost(2 * rows * rows * chunk, 2 * rows * chunk),
        name="score_sums",
    )(qk, *e_cells)
    scores = sum_steps(scores, "space", space_steps[:-1])
    scores = join(scores, "space", space_steps[-1], c_cells[first:first + 1])
    order = sorted(range(1, count), key=lambda s: (s & (s - 1) == 0, s))
    score_parts = [scores] + [swap(scores, s, count) for s in order]
    waited = score_parts[:1]
    pairs = pl.pallas_call(
        functools.partial(
            pair_kernel, me_of, count, main, half, per, length, group, channels, members
        ),
        out_shape=pair,
        in_specs=[whole] * (2 * count + 1) + [anywhere] * len(waited),
        out_specs=whole,
        compiler_params=params,
        cost_estimate=cost(2 * rows * rows * chunk, 4 * rows * chunk),
        name="pair_sums",
    )(ov, *e_cells, *c_cells, *waited)
    ahead = [pairs]
    outcome = pl.pallas_call(
        functools.partial(
            branch_kernel, me_of, count, main, half, per, group, channels, members, scale, len(ahead),
        ),
        out_shape=[pair] + [part] * count,
        in_specs=[whole] * (2 * count + 1) + [anywhere] * len(ahead),
        out_specs=[whole] * (count + 1),
        compiler_params=params,
        cost_estimate=cost(4 * rows * rows * chunk, 4 * rows * chunk),
        name="branch",
    )(ov, *score_parts, *e_cells, *ahead)
    scores, branch = outcome[0], outcome[1:]
    branch_home = exchange(branch)
    pairs = sum_steps(pairs, "space", space_steps[:-1])
    pairs = join(pairs, "space", space_steps[-1], branch_home[first:first + 1])
    pair_parts = [pairs] + [swap(pairs, s, count) for s in order]

    mid = (main + 1 + half) // 2
    weights, a_high, a_low, early = pl.pallas_call(
        functools.partial(
            early_gradient_kernel, me_of, count, main, per, mid, channels, members, group,
            scale,
        ),
        out_shape=[pair]
        + [jax.ShapeDtypeStruct((rows, rows), bf)] * 2
        + [jax.ShapeDtypeStruct((rows, mid * LANES), f32)],
        in_specs=[whole] * (count + 2),
        out_specs=[whole] * 4,
        compiler_params=params,
        cost_estimate=cost(10**8, 8 * rows * rows),
        name="early_gradient",
    )(scores, ovt, *c_cells)

    def gradient(begin, end, with_half, known, awaited, name):
        size = (end - begin) * LANES
        parts = pl.pallas_call(
            functools.partial(
                grad_kernel, me_of, count, main, with_half, per, group, channels, members, scale,
                begin, end, len(awaited), len(known) == 1,
            ),
            out_shape=[packed(end - begin, with_half)] * count,
            in_specs=[whole] * (3 * count + 3 + len(known)) + [anywhere] * len(awaited),
            out_specs=[whole] * count,
            compiler_params=params,
            cost_estimate=cost(8 * rows * rows * size, 6 * rows * size),
            name=name,
        )(weights, qk, qkt, *known, *e_cells, *c_cells, *pair_parts, *awaited)
        return exchange(parts)

    grad_a = gradient(0, mid, 0, [early], branch_home[1:], "input_gradient_a")
    grad_b = gradient(mid, main, half, [a_high, a_low], branch_home[1:], "input_gradient_b")
    serial = count * main - length // LANES > main - mid

    def finish(base, extra, stages, halves, before, after, name):
        slots = sum(len(stage) for stage in stages) + (count // 2 if halves else 0)
        waited = list(before) + list(after)
        return pl.pallas_call(
            functools.partial(
                finish_kernel, me_of, count, main, per, length, stages, halves, serial,
                len(waited), len(extra),
            ),
            out_shape=jax.ShapeDtypeStruct((per, length), f32),
            in_specs=[anywhere] * len(waited) + [whole] * (count + len(extra)),
            out_specs=in_hbm,
            scratch_shapes=[
                pltpu.VMEM((slots, per, mid * LANES), f32),
                pltpu.SemaphoreType.DMA((slots,)),
            ],
            input_output_aliases={0: 0} if before else {},
            compiler_params=params,
            cost_estimate=cost(per * length, 8 * per * length),
            name=name,
        )(*waited, *base, *extra)

    first_part = [(s, 0, mid, s, 0) for s in steps]
    updated = finish(
        e_mine, branch_home, [first_part, [(s, mid, main, s, 0) for s in steps]],
        [(s, main * per) for s in steps] if half else [], [], [grad_a[first]], "updated",
    )
    ensemble_grad = finish(
        c_mine, grad_a + grad_b[:1], [first_part, [(0, mid, main, count, mid)]],
        [], [], [], "ensemble_grad_early",
    )
    if count > 1:
        ensemble_grad = finish(
            c_mine, grad_b, [[(s, mid, main, s, mid) for s in steps[1:]]],
            [(s, (main - mid) * per) for s in steps] if half else [],
            [ensemble_grad], [], "ensemble_grad_late",
        )
    shape = (group, channels, length)
    return (updated.reshape(shape), ensemble_grad.reshape(shape))


def solution(mesh):
    split = P("mem", None, "space")
    return jax.shard_map(
        shards,
        mesh=mesh,
        in_specs=(split, split, P(), P(), P(), P()),
        out_specs=(split, split),
        check_vma=False,
    )
```

```python
import functools
import math

import jax
import jax.numpy as jnp
from jax import lax
from jax.experimental import pallas as pl
from jax.experimental.pallas import tpu as pltpu
from jax.sharding import PartitionSpec as P

LANES = 128
HIGH = lax.Precision.HIGHEST
VMEM = pltpu.MemorySpace.VMEM


def mm(a, b, dims, precision=None):
    return lax.dot_general(
        a, b, (dims, ((), ())), precision=precision, preferred_element_type=jnp.float32
    )


def chunk_start(index, chunk, length):
    return pl.multiple_of(jnp.minimum(index * chunk, length - chunk), LANES)


def partner(me, step):
    return me ^ step


def tile_layout(length, count):
    main, left = divmod(length // LANES, count)
    if left and 2 * left == count:
        return main, 1
    return main + (left > 0), 0


def tile_groups(first, last, half, most=4):
    tiles = list(range(first, last)) + [None] * half
    return [tiles[at:at + most] for at in range(0, len(tiles), most)]


def swap_halves(value):
    return pltpu.roll(value, LANES // 2, 1)


def left_half(shape):
    return lax.broadcasted_iota(jnp.int32, shape, 1) < LANES // 2


def pack(tile, odd=None):
    half = tile.shape[0] // 2
    top, low = tile[:half], tile[half:]
    left, right = top, swap_halves(low)
    if odd is not None:
        second = lax.broadcasted_iota(jnp.int32, top.shape, 1) * 0 + odd == 1
        left, right = jnp.where(second, swap_halves(top), top), jnp.where(second, low, right)
    return jnp.where(left_half(top.shape), left, right)


def tile_of(ref, tile, per, main):
    if tile is not None:
        return ref[tile * per:(tile + 1) * per, :]
    packed = ref[main * per:, :].astype(jnp.float32)
    return jnp.concatenate([packed, swap_halves(packed)], axis=0).astype(jnp.bfloat16)


def gather_tiles(refs, group, per, main):
    return jnp.concatenate(
        [
            jnp.concatenate([tile_of(ref, tile, per, main) for tile in group], axis=1)
            for ref in refs
        ],
        axis=0,
    )


def store_tiles(outs, value, group, per, first, last):
    for at, tile in enumerate(group):
        for s, out in enumerate(outs):
            rows = value[s * per:(s + 1) * per, at * LANES:(at + 1) * LANES]
            if tile is None:
                out[(last - first) * per:, :] = pack(rows).astype(jnp.bfloat16)
            else:
                out[(tile - first) * per:(tile - first + 1) * per, :] = rows.astype(
                    jnp.bfloat16
                )


def member_of_row(me, rows, channels, members, group):
    row = lax.broadcasted_iota(jnp.int32, (rows, members), 0)
    col = lax.broadcasted_iota(jnp.int32, (rows, members), 1)
    per_group = group * channels
    owner = (row // per_group) ^ me
    member = owner * group + (row % per_group) // channels
    return (member == col).astype(jnp.float32)


def split_kernel(me_of, steps, count, main, half, length, x_ref, *rest):
    outs = rest[-len(steps):]
    me = me_of()
    per = x_ref.shape[0]
    for out, s in zip(outs, steps):
        owner = partner(me, s)
        start = chunk_start(owner, main * LANES, length)
        for tile in range(main):
            place = pl.multiple_of(start + tile * LANES, LANES)
            out[tile * per:(tile + 1) * per, :] = x_ref[:, pl.ds(place, LANES)]
        if half:
            place = pl.multiple_of((main * count + owner // 2) * LANES, LANES)
            shared = x_ref[:, pl.ds(place, LANES)].astype(jnp.float32)
            out[main * per:, :] = pack(shared, owner % 2).astype(jnp.bfloat16)


def direct_split_kernel(me_of, steps, count, main, half, length, x_ref, *rest):
    outs, (held, shared, sem) = rest[:len(steps)], rest[len(steps):]
    me = me_of()
    per = x_ref.shape[0]
    copies = []
    for at, s in enumerate(steps):
        owner = partner(me, s)
        start = chunk_start(owner, main * LANES, length)
        copies.append(pltpu.make_async_copy(
            x_ref.at[:, pl.ds(start, main * LANES)], held.at[at], sem.at[2 * at]
        ))
        if half:
            place = pl.multiple_of((main * count + owner // 2) * LANES, LANES)
            copies.append(pltpu.make_async_copy(
                x_ref.at[:, pl.ds(place, LANES)], shared.at[at], sem.at[2 * at + 1]
            ))
    for copy in copies:
        copy.start()
    for copy in copies:
        copy.wait()
    for at, s in enumerate(steps):
        for tile in range(main):
            outs[at][tile * per:(tile + 1) * per, :] = held[
                at, :, tile * LANES:(tile + 1) * LANES
            ]
        if half:
            tile = shared[at].astype(jnp.float32)
            outs[at][main * per:, :] = pack(tile, partner(me, s) % 2).astype(jnp.bfloat16)


def tiled(small, rows, channels):
    tall = jnp.concatenate([small] * (rows // channels), axis=0)
    col = lax.broadcasted_iota(jnp.int32, (channels, rows), 1)
    row = lax.broadcasted_iota(jnp.int32, (channels, rows), 0)
    spread = (col % channels == row).astype(jnp.float32)
    return mm(tall, spread, ((1,), (0,)), HIGH)


def tiles_kernel(rows, channels, wq_ref, wk_ref, wv_ref, wo_ref, qk_ref, qkt_ref, ov_ref, ovt_ref):
    wq, wk = wq_ref[...].astype(jnp.float32), wk_ref[...].astype(jnp.float32)
    wv, wo = wv_ref[...].astype(jnp.float32), wo_ref[...].astype(jnp.float32)
    wqt, wkt, wvt, wot = wq.T, wk.T, wv.T, wo.T
    qk_ref[...] = tiled(mm(wqt, wk, ((1,), (0,)), HIGH), rows, channels)
    qkt_ref[...] = tiled(mm(wkt, wq, ((1,), (0,)), HIGH), rows, channels)
    ov_ref[...] = tiled(mm(wo, wv, ((1,), (0,)), HIGH), rows, channels)
    ovt_ref[...] = tiled(mm(wvt, wot, ((1,), (0,)), HIGH), rows, channels)


def three_parts(value):
    parts = []
    for _ in range(3):
        parts.append(value.astype(jnp.bfloat16))
        value = value - parts[-1].astype(jnp.float32)
    return parts


def fold(me, weighted, channels, members, group):
    rows = weighted.shape[0]
    half = jnp.sum(weighted.reshape(members, channels, rows), axis=1)
    picks = member_of_row(me, rows, channels, members, group).astype(jnp.bfloat16)
    half = sum(mm(part, picks, ((1,), (0,))) for part in three_parts(half))
    local = lax.broadcasted_iota(jnp.int32, (members, members), 1)
    member = lax.broadcasted_iota(jnp.int32, (members, members), 0)
    order = (((local // group) ^ me) * group + local % group == member).astype(jnp.bfloat16)
    return sum(mm(order, part, ((1,), (0,))) for part in three_parts(half))


def masked_gram(me, count, main, half, per, length, left, right):
    rows = count * per
    chunk = main * LANES
    skip = me * chunk - chunk_start(me, chunk, length)
    most = max(0, count * chunk - length)
    total = jnp.zeros((rows, rows), jnp.float32)
    at = 0
    for group in tile_groups(0, main, half):
        b = gather_tiles(right, group, per, main)
        a = b if left is right else gather_tiles(left, group, per, main)
        if at < most or None in group:
            lane = lax.broadcasted_iota(jnp.int32, a.shape, 1) + at
            valid = (lane >= skip) & (lane < chunk + LANES // 2)
            a = jnp.where(valid, a.astype(jnp.float32), 0.0).astype(jnp.bfloat16)
        total = total + mm(a, b, ((1,), (1,)))
        at += len(group) * LANES
    return total


def score_kernel(me_of, count, main, half, per, length, group, channels, members, tile_ref, *refs):
    me = me_of()
    fields, out_ref = refs[:count], refs[-1]
    total = masked_gram(me, count, main, half, per, length, fields, fields)
    out_ref[...] = fold(me, total * tile_ref[...], channels, members, group)


def pair_kernel(me_of, count, main, half, per, length, group, channels, members, tile_ref, *refs):
    me = me_of()
    fields, grads, out_ref = refs[:count], refs[count:2 * count], refs[-1]
    total = masked_gram(me, count, main, half, per, length, grads, fields)
    out_ref[...] = fold(me, total * tile_ref[...], channels, members, group)


def add_up(refs):
    return functools.reduce(jnp.add, [r[...] for r in refs])


def join_kernel(a_ref, b_ref, *refs):
    refs[-1][...] = a_ref[...] + b_ref[...]


def softmax(scores):
    peak = jnp.max(scores, axis=1, keepdims=True)
    exponent = jnp.exp(scores - peak)
    return exponent / jnp.sum(exponent, axis=1, keepdims=True)


def spread(small, picks):
    tall = mm(picks, small.astype(jnp.bfloat16), ((1,), (0,))).astype(jnp.bfloat16)
    return mm(tall, picks, ((1,), (1,)))


def spread_t(small, picks):
    tall = mm(picks, small.astype(jnp.bfloat16), ((1,), (1,))).astype(jnp.bfloat16)
    return mm(tall, picks, ((1,), (1,)))


def two_parts(value):
    high = value.astype(jnp.bfloat16)
    return high, (value - high.astype(jnp.float32)).astype(jnp.bfloat16)


def branch_kernel(
    me_of, count, main, half, per, group, channels, members, scale, waits, ov_ref, *refs
):
    me = me_of()
    sums, fields = refs[:count], refs[count:2 * count]
    total_ref, outs = refs[2 * count + waits], refs[2 * count + waits + 1:]
    rows = count * per
    total = add_up(sums)
    total_ref[...] = total
    picks = member_of_row(me, rows, channels, members, group).astype(jnp.bfloat16)
    weights = softmax(total * scale)
    high, low = two_parts(spread(weights, picks) * ov_ref[...])
    both = jnp.concatenate([high, low], axis=1)
    for tiles in tile_groups(0, main, half):
        e = gather_tiles(fields, tiles, per, main)
        value = mm(both, jnp.concatenate([e, e], axis=0), ((1,), (0,)))
        store_tiles(outs, value, tiles, per, 0, main)


def early_gradient_kernel(
    me_of, count, main, per, last, channels, members, group, scale, s_ref, ovt_ref, *refs
):
    grads, (w_ref, high_ref, low_ref, value_ref) = refs[:count], refs[count:]
    rows = ovt_ref.shape[0]
    picks = member_of_row(me_of(), rows, channels, members, group).astype(jnp.bfloat16)
    weights = softmax(s_ref[...] * scale)
    w_ref[...] = weights
    high, low = two_parts(spread_t(weights, picks) * ovt_ref[...])
    high_ref[...], low_ref[...] = high, low
    at = 0
    for tiles in tile_groups(0, last, 0):
        c = gather_tiles(grads, tiles, per, main)
        value_ref[:, at:at + len(tiles) * LANES] = mm(high, c, ((1,), (0,))) + mm(
            low, c, ((1,), (0,))
        )
        at += len(tiles) * LANES


def grad_kernel(
    me_of, count, main, half, per, group, channels, members, scale, first, last, waits, early,
    w_ref, qk_ref, qkt_ref, *refs,
):
    me = me_of()
    known, refs = refs[:1 if early else 2], refs[1 if early else 2:]
    fields, grads, sums = refs[:count], refs[count:2 * count], refs[2 * count:3 * count]
    outs = refs[3 * count + waits:]
    rows = count * per
    picks = member_of_row(me, rows, channels, members, group).astype(jnp.bfloat16)
    weights = w_ref[...]
    pairs = add_up(sums)
    slope = weights * (pairs - jnp.sum(weights * pairs, axis=1, keepdims=True)) * scale
    d_high, d_low = two_parts(
        spread(slope, picks) * qk_ref[...] + spread_t(slope, picks) * qkt_ref[...]
    )
    at = 0
    for tiles in tile_groups(first, last, half):
        e = gather_tiles(fields, tiles, per, main)
        value = mm(d_high, e, ((1,), (0,))) + mm(d_low, e, ((1,), (0,)))
        if early:
            value = value + known[0][:, at:at + len(tiles) * LANES]
        else:
            c = gather_tiles(grads, tiles, per, main)
            for weight in known:
                value = value + mm(weight[...], c, ((1,), (0,)))
        store_tiles(outs, value, tiles, per, first, last)
        at += len(tiles) * LANES


def finish_kernel(
    me_of, count, main, per, length, stages, halves, serial, waits, extras, *refs
):
    me = me_of()
    base, extra = refs[waits:waits + count], refs[waits + count:waits + count + extras]
    out_ref, held, sem = refs[waits + count + extras:]

    def send(slot, size, place):
        place = pl.multiple_of(place, LANES)
        copy = pltpu.make_async_copy(
            held.at[slot, :, pl.ds(0, size)], out_ref.at[:, pl.ds(place, size)], sem.at[slot]
        )
        copy.start()
        if serial:
            copy.wait()
        return copy

    slot = 0
    for number, stage in enumerate(stages):
        copies = []
        for s, begin, end, index, origin in stage:
            for tile in range(begin, end):
                mine = base[s][tile * per:(tile + 1) * per, :].astype(jnp.float32)
                more = extra[index][(tile - origin) * per:(tile - origin + 1) * per, :]
                held[slot, :, (tile - begin) * LANES:(tile - begin + 1) * LANES] = (
                    mine + more.astype(jnp.float32)
                )
            start = chunk_start(partner(me, s), main * LANES, length)
            copies.append(send(slot, (end - begin) * LANES, start + begin * LANES))
            slot += 1
        if halves and number == len(stages) - 1:
            packed = [
                base[s][main * per:, :].astype(jnp.float32)
                + extra[index][row:, :].astype(jnp.float32)
                for s, (index, row) in enumerate(halves)
            ]
            shape = packed[0].shape
            odd = lax.broadcasted_iota(jnp.int32, shape, 1) * 0 + me % 2 == 1
            for s in range(0, count, 2):
                even_part = jnp.where(odd, packed[s + 1], packed[s])
                odd_part = jnp.where(odd, packed[s], packed[s + 1])
                left = left_half(shape)
                held[slot, :per // 2, :LANES] = jnp.where(
                    left, even_part, swap_halves(odd_part)
                )
                held[slot, per // 2:, :LANES] = jnp.where(
                    left, swap_halves(even_part), odd_part
                )
                place = (main * count + partner(me, s) // 2) * LANES
                copies.append(send(slot, LANES, place))
                slot += 1
        if not serial:
            for copy in copies:
                copy.wait()


def swap(value, step, count):
    return lax.ppermute(value, "mem", [(i, i ^ step) for i in range(count)])


def exchange(parts):
    count = len(parts)
    return [part if s == 0 else swap(part, s, count) for s, part in enumerate(parts)]


def sum_steps(value, name, steps):
    size = lax.axis_size(name)
    for step in steps:
        value = value + lax.ppermute(value, name, [(i, i ^ step) for i in range(size)])
    return value


def doubling(size):
    steps, step = [], 1
    while step < size:
        steps.append(step)
        step *= 2
    return steps


def shards(ensemble, cotangent, w_query, w_key, w_value, w_out):
    count = lax.axis_size("mem")
    group, channels, length = ensemble.shape
    members = group * count
    per = group * channels
    rows = per * count
    main, half = tile_layout(length, count)
    chunk = main * LANES + half * LANES // 2
    scale = 1.0 / (length * lax.axis_size("space") * math.sqrt(channels))
    me_of = lambda: lax.axis_index("mem")
    bf, f32 = jnp.bfloat16, jnp.float32
    whole = pl.BlockSpec(memory_space=VMEM)
    anywhere = pl.BlockSpec(memory_space=pl.ANY)
    in_hbm = pl.BlockSpec(memory_space=pltpu.MemorySpace.HBM)
    params = pltpu.CompilerParams(vmem_limit_bytes=16 * 1024 * 1024 + 24 * rows * rows)

    def packed(tiles, with_half):
        return jax.ShapeDtypeStruct((tiles * per + with_half * per // 2, LANES), bf)

    part = packed(main, half)
    square = jax.ShapeDtypeStruct((rows, rows), f32)
    pair = jax.ShapeDtypeStruct((members, members), f32)
    fields = ensemble.reshape(per, length)
    grads = cotangent.reshape(per, length)

    def cost(flops, moved):
        return pl.CostEstimate(flops=flops, bytes_accessed=moved, transcendentals=0)

    first = min(1, count - 1)

    def split(operands, steps, name):
        return pl.pallas_call(
            functools.partial(split_kernel, me_of, steps, count, main, half, length),
            out_shape=[part] * len(steps),
            in_specs=[whole] + [anywhere] * (len(operands) - 1),
            out_specs=[whole] * len(steps),
            compiler_params=params,
            name=name,
        )(*operands)

    steps = list(range(count))
    ends = sorted({0, count - 1})
    middle = steps[1:-1]
    near = []
    if middle:
        near = list(pl.pallas_call(
            functools.partial(
                direct_split_kernel, me_of, middle, count, main, half, length
            ),
            out_shape=[part] * len(middle),
            in_specs=[in_hbm],
            out_specs=[whole] * len(middle),
            scratch_shapes=[
                pltpu.VMEM((len(middle), per, main * LANES), bf),
                pltpu.VMEM((len(middle), per, LANES), bf),
                pltpu.SemaphoreType.DMA((2 * len(middle),)),
            ],
            compiler_params=params,
            name="split_fields_near",
        )(pltpu.with_memory_space_constraint(fields, pltpu.HBM)))
    far = list(split([fields] + near[:1], ends, "split_fields_far"))
    e_mine = far[:1] + near + far[1:]
    e_cells = exchange(e_mine)
    qk, qkt, ov, ovt = pl.pallas_call(
        functools.partial(tiles_kernel, rows, channels),
        out_shape=[square] * 4,
        in_specs=[whole] * 4,
        out_specs=[whole] * 4,
        compiler_params=params,
        cost_estimate=cost(10**8, 4 * 4 * rows * rows),
        name="weight_tiles",
    )(w_query, w_key, w_value, w_out)
    c_mine = split([grads, e_cells[first], qk], steps, "split_grads")
    c_cells = exchange(c_mine)
    space_steps = doubling(lax.axis_size("space"))

    def join(value, name, step, waited):
        size = lax.axis_size(name)
        other = lax.ppermute(value, name, [(i, i ^ step) for i in range(size)])
        return pl.pallas_call(
            join_kernel,
            out_shape=pair,
            in_specs=[whole] * 2 + [anywhere] * len(waited),
            out_specs=whole,
            compiler_params=params,
            cost_estimate=cost(members * members, 12 * members * members),
            name="join_sums",
        )(value, other, *waited)

    scores = pl.pallas_call(
        functools.partial(
            score_kernel, me_of, count, main, half, per, length, group, channels, members
        ),
        out_shape=pair,
        in_specs=[whole] * (count + 1),
        out_specs=whole,
        compiler_params=params,
        cost_estimate=cost(2 * rows * rows * chunk, 2 * rows * chunk),
        name="score_sums",
    )(qk, *e_cells)
    scores = sum_steps(scores, "space", space_steps[:-1])
    scores = join(scores, "space", space_steps[-1], c_cells[first:first + 1])
    order = sorted(range(1, count), key=lambda s: (s & (s - 1) == 0, s))
    score_parts = [scores] + [swap(scores, s, count) for s in order]
    waited = score_parts[:1]
    pairs = pl.pallas_call(
        functools.partial(
            pair_kernel, me_of, count, main, half, per, length, group, channels, members
        ),
        out_shape=pair,
        in_specs=[whole] * (2 * count + 1) + [anywhere] * len(waited),
        out_specs=whole,
        compiler_params=params,
        cost_estimate=cost(2 * rows * rows * chunk, 4 * rows * chunk),
        name="pair_sums",
    )(ov, *e_cells, *c_cells, *waited)
    ahead = [pairs]
    outcome = pl.pallas_call(
        functools.partial(
            branch_kernel, me_of, count, main, half, per, group, channels, members, scale, len(ahead),
        ),
        out_shape=[pair] + [part] * count,
        in_specs=[whole] * (2 * count + 1) + [anywhere] * len(ahead),
        out_specs=[whole] * (count + 1),
        compiler_params=params,
        cost_estimate=cost(4 * rows * rows * chunk, 4 * rows * chunk),
        name="branch",
    )(ov, *score_parts, *e_cells, *ahead)
    scores, branch = outcome[0], outcome[1:]
    branch_home = exchange(branch)
    pairs = sum_steps(pairs, "space", space_steps[:-1])
    pairs = join(pairs, "space", space_steps[-1], branch_home[first:first + 1])
    pair_parts = [pairs] + [swap(pairs, s, count) for s in order]

    mid = (main + 1 + half) // 2
    weights, a_high, a_low, early = pl.pallas_call(
        functools.partial(
            early_gradient_kernel, me_of, count, main, per, mid, channels, members, group,
            scale,
        ),
        out_shape=[pair]
        + [jax.ShapeDtypeStruct((rows, rows), bf)] * 2
        + [jax.ShapeDtypeStruct((rows, mid * LANES), f32)],
        in_specs=[whole] * (count + 2),
        out_specs=[whole] * 4,
        compiler_params=params,
        cost_estimate=cost(10**8, 8 * rows * rows),
        name="early_gradient",
    )(scores, ovt, *c_cells)

    def gradient(begin, end, with_half, known, awaited, name):
        size = (end - begin) * LANES
        parts = pl.pallas_call(
            functools.partial(
                grad_kernel, me_of, count, main, with_half, per, group, channels, members, scale,
                begin, end, len(awaited), len(known) == 1,
            ),
            out_shape=[packed(end - begin, with_half)] * count,
            in_specs=[whole] * (3 * count + 3 + len(known)) + [anywhere] * len(awaited),
            out_specs=[whole] * count,
            compiler_params=params,
            cost_estimate=cost(8 * rows * rows * size, 6 * rows * size),
            name=name,
        )(weights, qk, qkt, *known, *e_cells, *c_cells, *pair_parts, *awaited)
        return exchange(parts)

    grad_a = gradient(0, mid, 0, [early], branch_home[1:], "input_gradient_a")
    grad_b = gradient(mid, main, half, [a_high, a_low], branch_home[1:], "input_gradient_b")
    serial = count * main - length // LANES > main - mid

    def finish(base, extra, stages, halves, before, after, name):
        slots = sum(len(stage) for stage in stages) + (count // 2 if halves else 0)
        waited = list(before) + list(after)
        return pl.pallas_call(
            functools.partial(
                finish_kernel, me_of, count, main, per, length, stages, halves, serial,
                len(waited), len(extra),
            ),
            out_shape=jax.ShapeDtypeStruct((per, length), f32),
            in_specs=[anywhere] * len(waited) + [whole] * (count + len(extra)),
            out_specs=in_hbm,
            scratch_shapes=[
                pltpu.VMEM((slots, per, mid * LANES), f32),
                pltpu.SemaphoreType.DMA((slots,)),
            ],
            input_output_aliases={0: 0} if before else {},
            compiler_params=params,
            cost_estimate=cost(per * length, 8 * per * length),
            name=name,
        )(*waited, *base, *extra)

    first_part = [(s, 0, mid, s, 0) for s in steps]
    updated = finish(
        e_mine, branch_home, [first_part, [(s, mid, main, s, 0) for s in steps]],
        [(s, main * per) for s in steps] if half else [], [], [grad_a[first]], "updated",
    )
    ensemble_grad = finish(
        c_mine, grad_a + grad_b[:1], [first_part, [(0, mid, main, count, mid)]],
        [], [], [], "ensemble_grad_early",
    )
    if count > 1:
        ensemble_grad = finish(
            c_mine, grad_b, [[(s, mid, main, s, mid) for s in steps[1:]]],
            [(s, (main - mid) * per) for s in steps] if half else [],
            [ensemble_grad], [], "ensemble_grad_late",
        )
    shape = (group, channels, length)
    return (updated.reshape(shape), ensemble_grad.reshape(shape))


def solution(mesh):
    split = P("mem", None, "space")
    return jax.shard_map(
        shards,
        mesh=mesh,
        in_specs=(split, split, P(), P(), P(), P()),
        out_specs=(split, split),
        check_vma=False,
    )
```
